32 devices in a mesh: parts: 2 (over y), rows: 4 (over z), cols: 2 (over x), sub: 2 (over core).
Axes of the slice: x: 2, y: 2, z: 4, core: 2. Of those that a mesh axis runs over, the one named last changes fastest.
Arguments:
- right_side: float32 [128, 8192], P(('parts', 'cols'), ('rows', 'sub')), parts along dimension 0, may hold values from -6 to 6
- start_field: float32 [128, 8192], P(('parts', 'cols'), ('rows', 'sub')), parts along dimension 0, may hold values from -4 to 4
- fine_tiles: bfloat16 [128, 3, 128, 128], P(('parts', 'rows', 'sub')), parts along dimension 0, as said below
- fine_links: int32 [128, 3], P(('parts', 'rows', 'sub')), parts along dimension 0, may hold values from 0 to 9, as said below
- fine_groups: int32 [16384], P(('parts', 'rows', 'sub')), parts along dimension 0, may hold values from 0 to 511, as said below
- mid_tiles: bfloat16 [8, 3, 128, 128], P('parts'), parts along dimension 0, as said below
- mid_links: int32 [8, 3], P('parts'), parts along dimension 0, may hold values from 0 to 3, as said below
- mid_groups: int32 [1024], P('parts'), parts along dimension 0, may hold values from 0 to 255
- last_inverse: float32 [512, 256], P('parts'), parts along dimension 0
Outputs:
- solution: float32 [128, 8192], P(('parts', 'cols'), ('rows', 'sub')), parts along dimension 0
The draws below stay inside these ranges and needn't reach their ends.
There are 2 independent parts, one for each index of `parts`. The reference program is written for one: setup_inputs(seed, part) draws one part's arguments, and reference() takes and returns one part's arrays. A program takes and returns all parts, laid end to end along the dimension named above; each array names one. Nothing has to cross between parts.
Inputs may be any that keep to these rules, and one draw needn't show every extreme that they name: `fine_links`: entry 0 of fine block row g is g % 8 + 1, the row's own block; entry 1 of every row with g % 8 = 0 is 0 and entry 2 of every row with g % 8 = 7 is 9. `fine_groups`: fine cell c belongs to a middle cell from w * (c // 1024) to w * (c // 1024) + w - 1, where w = 64. `mid_links`: entry 0 of middle block row g is g. `fine_tiles`: the diagonal of each tile [g, 0] exceeds the sum of magnitudes of the rest of its row by 0.1 or more; all other entries are at most 0. `mid_tiles`: as for fine_tiles, with every entry 16 times larger.
All inputs are finite; a program needn't handle non-finite values.
Results may differ from the reference program's by a relative error of at most 0.0003.
The reference program's roundings to bfloat16 on the way count: a program that leaves them out, or rounds other values in their place, can miss the bound.
Values may be sent and summed in bfloat16 or wider, within the bound.
A program may use at most 64 MiB of HBM per device.

```python
import jax
import jax.numpy as jnp
from jax import lax

TILE = 128
B0 = 8
K0 = 3
K1 = 3
N2 = 256
SCEN = 64
B1 = 4
FBLOCKS = 64
N0 = 8192
N1 = 512
AGG = 16
AGG2 = 2


def tile_law(key, blocks, links, size, power, low, high, factor):
    key_off, key_diag = jax.random.split(key)
    raw = jax.random.uniform(key_off, (blocks, links, size, size), jnp.float32) ** power
    slot = jnp.arange(links, dtype=jnp.int32)
    weights = jnp.where(slot == 0, 0.5, (links - 0.5) / (links - 1.0)).astype(jnp.float32)
    entries = -raw * weights[None, :, None, None] / (size * links)
    diag_values = jax.random.uniform(key_diag, (blocks, size), jnp.float32, low, high)
    identity = jnp.eye(size, dtype=jnp.float32)
    first = entries[:, 0] * (1.0 - identity)[None] + identity[None] * diag_values[:, :, None]
    entries = entries.at[:, 0].set(first)
    return entries * factor


def draw_fine_tiles(key, part):
    key = jax.random.fold_in(key, 3)
    return tile_law(key, FBLOCKS, K0, TILE, 0.25, 1.15, 1.45, 1.0).astype(jnp.bfloat16)


def draw_mid_tiles(key, part):
    key = jax.random.fold_in(key, 5)
    return tile_law(key, B1, K1, TILE, 0.25, 1.15, 1.45, float(AGG)).astype(jnp.bfloat16)


def draw_fine_links(key, part):
    key = jax.random.fold_in(key, 7)
    picks = jax.random.randint(key, (FBLOCKS, K0), 0, B0 + 2).astype(jnp.int32)
    local = (jnp.arange(FBLOCKS, dtype=jnp.int32) % B0).astype(jnp.int32)
    picks = picks.at[:, 0].set(local + 1)
    picks = picks.at[:, 1].set(jnp.where(local == 0, 0, picks[:, 1]).astype(jnp.int32))
    picks = picks.at[:, 2].set(jnp.where(local == B0 - 1, B0 + 1, picks[:, 2]).astype(jnp.int32))
    return picks


def draw_fine_groups(key, part):
    key = jax.random.fold_in(key, 11)
    window = N1 * B0 // FBLOCKS
    owner = (jnp.arange(N0, dtype=jnp.int32) // (B0 * TILE)).astype(jnp.int32)
    picks = jax.random.randint(key, (N0,), 0, window).astype(jnp.int32)
    picks = picks.at[0].set(0)
    picks = picks.at[N0 - 1].set(window - 1)
    return (owner * window + picks).astype(jnp.int32)


def draw_mid_links(key, part):
    key = jax.random.fold_in(key, 9)
    picks = jax.random.randint(key, (B1, K1), 0, B1).astype(jnp.int32)
    picks = picks.at[:, 0].set(jnp.arange(B1, dtype=jnp.int32))
    picks = picks.at[0, 1].set(B1 - 1)
    return picks


def draw_last_inverse(key, part):
    key = jax.random.fold_in(key, 13)
    key_off, key_diag = jax.random.split(key)
    spread = jax.random.normal(key_off, (N2, N2), jnp.float32) * (0.3 / N2 ** 0.5)
    diag_values = jax.random.uniform(key_diag, (N2,), jnp.float32, 0.5, 1.0)
    identity = jnp.eye(N2, dtype=jnp.float32)
    matrix = spread * (1.0 - identity) + identity * diag_values[None, :]
    return matrix / float(AGG * AGG2)


def place_ends(array, rng, smallest, high):
    index_at = [jax.random.randint(jax.random.fold_in(rng, axis), (), 0, length) for axis, length in enumerate(array.shape)]
    longest = array.shape.index(max(array.shape))
    next_to = index_at[:longest] + [(index_at[longest] + 1) % array.shape[longest]] + index_at[longest + 1:]
    return array.at[tuple(index_at)].set(smallest).at[tuple(next_to)].set(high)


def steps_of(stream_key, extent, pieces, low, top_value):
    def one(axis_at, parts):
        heights = jax.random.uniform(jax.random.fold_in(jax.random.fold_in(stream_key, 6), axis_at), (parts,), jnp.float32, low / len(pieces), top_value / len(pieces))
        return jnp.repeat(jnp.exp(heights), extent[axis_at] // parts).reshape((-1,) + (1,) * (len(extent) - axis_at - 1))

    loudness = one(*pieces[0])
    for cut in pieces[1:]:
        loudness = loudness * one(*cut)
    return loudness


def scatter_about(stream_key, dims, scale, reach, shards=(), kind=jnp.bfloat16):
    values = scale * jax.random.normal(stream_key, dims, jnp.float32)
    if shards:
        values = values * steps_of(stream_key, dims, shards, -0.22, 0.18)
    return jnp.clip(values, -reach, reach).astype(kind)


def setup_inputs(seed: int = 0, part: int = 0) -> dict:
    keys = jax.random.split(jax.random.key(seed), 10)
    own_keys = jax.random.split(jax.random.fold_in(keys[9], part), 10)
    return {
        "right_side": scatter_about(own_keys[0], (SCEN, N0), 1.0, 6.0, ((0, 2), (1, 8)), jnp.float32),
        "start_field": scatter_about(own_keys[1], (SCEN, N0), 0.5, 4.0, ((0, 2), (1, 8)), jnp.float32),
        "fine_tiles": draw_fine_tiles(jax.random.fold_in(jax.random.fold_in(keys[9], part), 71), part),
        "fine_links": draw_fine_links(jax.random.fold_in(jax.random.fold_in(keys[9], part), 71), part),
        "fine_groups": draw_fine_groups(jax.random.fold_in(jax.random.fold_in(keys[9], part), 71), part),
        "mid_tiles": draw_mid_tiles(jax.random.fold_in(jax.random.fold_in(keys[9], part), 71), part),
        "mid_links": draw_mid_links(jax.random.fold_in(jax.random.fold_in(keys[9], part), 71), part),
        "mid_groups": place_ends(jax.random.randint(own_keys[7], (N1,), 0, N2), jax.random.fold_in(own_keys[7], 1), 0, N2 - 1).astype(jnp.int32),
        "last_inverse": draw_last_inverse(jax.random.fold_in(jax.random.fold_in(keys[9], part), 71), part),
    }


damping = 0.6


def fine_apply(field, fine_tiles, fine_links):
    rounded = field.astype(jnp.bfloat16).reshape(SCEN, FBLOCKS, TILE)
    padded = jnp.pad(rounded, ((0, 0), (1, 1), (0, 0)))
    base = (jnp.arange(FBLOCKS, dtype=jnp.int32) // B0) * B0
    index = (base[:, None] + fine_links).astype(jnp.int32)
    picked = padded[:, index].astype(jnp.float32)
    result = jnp.einsum("snkc,nkrc->snr", picked, fine_tiles.astype(jnp.float32))
    return result.reshape(SCEN, N0)


def mid_apply(field, mid_tiles, mid_links):
    rounded = field.astype(jnp.bfloat16).reshape(field.shape[0], B1, TILE)
    picked = rounded[:, mid_links].astype(jnp.float32)
    result = jnp.einsum("snkc,nkrc->snr", picked, mid_tiles.astype(jnp.float32))
    return result.reshape(field.shape[0], N1)


def reference(right_side, start_field, fine_tiles, fine_links, fine_groups, mid_tiles, mid_links, mid_groups, last_inverse):
    fine_diag = jnp.diagonal(fine_tiles[:, 0].astype(jnp.float32), axis1=1, axis2=2).reshape(N0)
    mid_diag = jnp.diagonal(mid_tiles[:, 0].astype(jnp.float32), axis1=1, axis2=2).reshape(N1)
    field = start_field
    for sweep in range(2):
        field = field + damping * (right_side - fine_apply(field, fine_tiles, fine_links)) / fine_diag
    fine_resid = right_side - fine_apply(field, fine_tiles, fine_links)
    mid_side = jnp.zeros((SCEN, N1), jnp.float32).at[:, fine_groups].add(fine_resid)
    mid_field = jnp.zeros((SCEN, N1), jnp.float32)
    for sweep in range(2):
        mid_field = mid_field + damping * (mid_side - mid_apply(mid_field, mid_tiles, mid_links)) / mid_diag
    mid_resid = mid_side - mid_apply(mid_field, mid_tiles, mid_links)
    last_side = jnp.zeros((SCEN, N2), jnp.float32).at[:, mid_groups].add(mid_resid)
    last_fix = jnp.dot(last_side, last_inverse.T, precision=lax.Precision.HIGHEST)
    mid_field = mid_field + last_fix[:, mid_groups]
    for sweep in range(2):
        mid_field = mid_field + damping * (mid_side - mid_apply(mid_field, mid_tiles, mid_links)) / mid_diag
    field = field + mid_field[:, fine_groups]
    for sweep in range(2):
        field = field + damping * (right_side - fine_apply(field, fine_tiles, fine_links)) / fine_diag
    return field
```

```python
import functools

import jax
import jax.numpy as jnp
from jax import lax
from jax.experimental import pallas as pl
from jax.experimental.pallas import tpu as pltpu
from jax.sharding import PartitionSpec as P

damping = 0.6
MESH = pl.DeviceIdType.MESH
F32 = jnp.float32
BF16 = jnp.bfloat16


def dot_nt(a, b):
    return lax.dot_general(a, b, (((1,), (1,)), ((), ())), preferred_element_type=F32)


def dot_nn(a, b):
    return lax.dot_general(a, b, (((1,), (0,)), ((), ())), preferred_element_type=F32)


def pieces(x, count):
    out = []
    for _ in range(count):
        high = x.astype(BF16)
        out.append(high)
        x = x - high.astype(F32)
    return jnp.concatenate(out, axis=0)


def unstack(y, count):
    rows = y.shape[0] // count
    total = y[(count - 1) * rows :]
    for i in range(count - 2, -1, -1):
        total = y[i * rows : (i + 1) * rows] + total
    return total


def one_hot_t(groups, base, rows):
    ids = lax.broadcasted_iota(jnp.int32, (rows, groups.shape[1]), 0) + base
    return jnp.where(ids == groups, 1.0, 0.0).astype(BF16)


def scale_of(tile):
    size = tile.shape[0]
    row = lax.broadcasted_iota(jnp.int32, (size, size), 0)
    col = lax.broadcasted_iota(jnp.int32, (size, size), 1)
    return damping / jnp.sum(jnp.where(row == col, tile.astype(F32), 0.0), axis=0, keepdims=True)


def kernel(
    n,
    sub,
    links,
    mid_links,
    b_any,
    u_any,
    t_any,
    grp_any,
    mt_any,
    mg_any,
    li_any,
    out_ref,
    b_v,
    u_v,
    t_v,
    grp_v,
    mt_v,
    mg_v,
    li_v,
    xb0,
    xb1,
    xb2,
    xb3,
    xb4,
    halo_f,
    ends_f,
    grp_h,
    slabs,
    pt,
    ct,
    e_hi,
    e_lo,
    mb,
    mid_v,
    load_sem,
    halo_send,
    halo_recv,
    all_send,
    all_recv,
):
    blocks, tile = t_v.shape[0], t_v.shape[2]
    mid_blocks = mt_v.shape[0]
    last = li_v.shape[0]
    per = n // mid_blocks
    me = lax.axis_index("rows") * sub + lax.axis_index("sub")
    has_left = me > 0
    has_right = me < n - 1

    def place(j):
        return {"rows": lax.div(j, sub), "sub": lax.rem(j, sub)}

    loads = [
        pltpu.make_async_copy(src, dst, load_sem.at[i])
        for i, (src, dst) in enumerate(
            (
                (u_any, u_v),
                (grp_any, grp_v),
                (t_any, t_v),
                (b_any, b_v),
                (mg_any, mg_v),
                (li_any, li_v),
                (mt_any, mt_v),
            )
        )
    ]
    for load in loads:
        load.start()

    barrier = pltpu.get_barrier_semaphore()
    for off in range(1, n):
        pl.semaphore_signal(
            barrier, inc=1, device_id=place(lax.rem(me + off, n)), device_id_type=MESH
        )

    left = jnp.maximum(me - 1, 0)
    right = jnp.minimum(me + 1, n - 1)

    def to_left(i, src, dst):
        return pltpu.make_async_remote_copy(
            src_ref=src,
            dst_ref=dst,
            send_sem=halo_send.at[i, 0],
            recv_sem=halo_recv.at[i, 1],
            device_id=place(left),
            device_id_type=MESH,
        )

    def to_right(i, src, dst):
        return pltpu.make_async_remote_copy(
            src_ref=src,
            dst_ref=dst,
            send_sem=halo_send.at[i, 1],
            recv_sem=halo_recv.at[i, 0],
            device_id=place(right),
            device_id_type=MESH,
        )

    def pair(i, first, final, before, after):
        return to_left(i, first, after), to_right(i, final, before)

    def ends(i, xb):
        return pair(i, xb.at[1], xb.at[blocks], xb.at[0], xb.at[blocks + 1])

    swaps = [
        ends(0, xb0),
        ends(1, xb1),
        pair(2, ends_f.at[0], ends_f.at[1], halo_f.at[0], halo_f.at[1]),
        ends(3, xb4),
        pair(4, grp_v, grp_v, grp_h.at[0], grp_h.at[1]),
    ]

    def send(i):
        @pl.when(has_left)
        def _():
            swaps[i][0].start()

        @pl.when(has_right)
        def _():
            swaps[i][1].start()

    def recv(i):
        @pl.when(has_left)
        def _():
            swaps[i][1].wait_recv()

        @pl.when(has_right)
        def _():
            swaps[i][0].wait_recv()

    def sent(i):
        @pl.when(has_left)
        def _():
            swaps[i][0].wait_send()

        @pl.when(has_right)
        def _():
            swaps[i][1].wait_send()

    zero_b = jnp.zeros(xb0.shape[1:], BF16)
    zero_f = jnp.zeros(halo_f.shape[1:], F32)

    @pl.when(me == 0)
    def _():
        for xb in (xb0, xb1, xb4):
            xb[0] = zero_b
        halo_f[0] = zero_f
        grp_h[0] = jnp.zeros(grp_h.shape[1:], jnp.int32)

    @pl.when(me == n - 1)
    def _():
        for xb in (xb0, xb1, xb4):
            xb[blocks + 1] = zero_b
        halo_f[1] = zero_f
        grp_h[1] = jnp.zeros(grp_h.shape[1:], jnp.int32)

    order = [0, blocks - 1] + list(range(1, blocks - 1))
    cells = [slice(g * tile, (g + 1) * tile) for g in range(blocks)]

    loads[0].wait()
    for g in order:
        xb0[g + 1] = u_v[:, cells[g]].astype(BF16)
    loads[1].wait()
    pl.semaphore_wait(barrier, n - 1)
    send(0)
    send(4)

    def own(xb):
        return [dot_nt(xb[g + 1], t_v[g, 0]) for g in range(blocks)]

    def rest(xb, g):
        picked = jnp.concatenate([xb[links[g, 1]], xb[links[g, 2]]], axis=1)
        return dot_nt(picked, jnp.concatenate([t_v[g, 1], t_v[g, 2]], axis=1))

    loads[2].wait()
    loads[3].wait()
    acc = own(xb0)
    scale = [scale_of(t_v[g, 0]) for g in range(blocks)]
    base = lax.div(me, per) * tile
    for g in range(blocks):
        pt[:, cells[g]] = one_hot_t(grp_v[g : g + 1], base, tile)

    recv(0)
    for g in order:
        new = u_v[:, cells[g]] + (b_v[:, cells[g]] - (acc[g] + rest(xb0, g))) * scale[g]
        u_v[:, cells[g]] = new
        xb1[g + 1] = new.astype(BF16)
        if g == blocks - 1:
            send(1)
    acc = own(xb1)

    for i in (4, 5, 6):
        loads[i].wait()
    flipped = li_v[...].T
    flipped_hi = flipped.astype(BF16)
    flipped_lo = (flipped - flipped_hi.astype(F32)).astype(BF16)
    for m in range(mid_blocks):
        hot = one_hot_t(mg_v[m : m + 1], 0, last)
        ct[m] = hot
        e_hi[m] = dot_nn(flipped_hi, hot).astype(BF16)
        e_lo[m] = dot_nn(flipped_lo, hot).astype(BF16)

    recv(1)
    for g in order:
        new = u_v[:, cells[g]] + (b_v[:, cells[g]] - (acc[g] + rest(xb1, g))) * scale[g]
        u_v[:, cells[g]] = new
        xb2[g + 1] = new.astype(BF16)
        if g == 0:
            ends_f[0] = new
        if g == blocks - 1:
            ends_f[1] = new
            send(2)
    acc = own(xb2)
    mid_scale = [scale_of(mt_v[m, 0]) for m in range(mid_blocks)]

    recv(2)
    xb2[0] = halo_f[0].astype(BF16)
    xb2[blocks + 1] = halo_f[1].astype(BF16)
    resid = jnp.concatenate(
        [pieces(b_v[:, cells[g]] - (acc[g] + rest(xb2, g)), 3) for g in range(blocks)], axis=1
    )
    slabs[me] = unstack(dot_nt(resid, pt[...]), 3)
    gathers = []
    for off in range(n - 1, 0, -1):
        copy = pltpu.make_async_remote_copy(
            src_ref=slabs.at[me],
            dst_ref=slabs.at[me],
            send_sem=all_send.at[off - 1],
            recv_sem=all_recv.at[off - 1],
            device_id=place(lax.rem(me + off, n)),
            device_id_type=MESH,
        )
        copy.start()
        gathers.append(copy)
    recv(4)
    hot_left = one_hot_t(grp_h[0, blocks - 1 : blocks], lax.div(left, per) * tile, tile)
    hot_right = one_hot_t(grp_h[1, 0:1], lax.div(right, per) * tile, tile)
    for copy in gathers:
        copy.wait_recv()

    side = []
    for m in range(mid_blocks):
        total = slabs[m * per]
        for i in range(1, per):
            total = total + slabs[m * per + i]
        side.append(total)

    def mid_apply(values):
        for m in range(mid_blocks):
            mb[m] = values[m].astype(BF16)
        out = []
        for m in range(mid_blocks):
            picked = jnp.concatenate(
                [mb[m], mb[mid_links[m, 1]], mb[mid_links[m, 2]]], axis=1
            )
            out.append(
                dot_nt(picked, jnp.concatenate([mt_v[m, 0], mt_v[m, 1], mt_v[m, 2]], axis=1))
            )
        return out

    def mid_sweep(values):
        return [
            v + (s - a) * d for v, s, a, d in zip(values, side, mid_apply(values), mid_scale)
        ]

    mid = [s * d for s, d in zip(side, mid_scale)]
    mid = mid_sweep(mid)
    mid_resid = [s - a for s, a in zip(side, mid_apply(mid))]
    last_side = dot_nt(pieces(mid_resid[0], 2), ct[0])
    for m in range(1, mid_blocks):
        last_side = last_side + dot_nt(pieces(mid_resid[m], 2), ct[m])
    both = pieces(unstack(last_side, 2), 2)
    high = both[: both.shape[0] // 2]
    mid = [
        mid[m] + (unstack(dot_nn(both, e_hi[m]), 2) + dot_nn(high, e_lo[m]))
        for m in range(mid_blocks)
    ]
    mid = mid_sweep(mid)
    mid = mid_sweep(mid)
    for m in range(mid_blocks):
        mid_v[m] = mid[m]

    def lift(device, hot):
        return unstack(dot_nn(pieces(mid_v[lax.div(device, per)], 3), hot), 3)

    add = lift(me, pt[...])
    before = halo_f[0] + lift(left, hot_left)
    after = halo_f[1] + lift(right, hot_right)
    xb3[0] = jnp.where(has_left, before, 0.0).astype(BF16)
    xb3[blocks + 1] = jnp.where(has_right, after, 0.0).astype(BF16)
    for g in range(blocks):
        new = u_v[:, cells[g]] + add[:, cells[g]]
        u_v[:, cells[g]] = new
        xb3[g + 1] = new.astype(BF16)

    acc = own(xb3)
    for g in order:
        new = u_v[:, cells[g]] + (b_v[:, cells[g]] - (acc[g] + rest(xb3, g))) * scale[g]
        u_v[:, cells[g]] = new
        xb4[g + 1] = new.astype(BF16)
        if g == blocks - 1:
            send(3)
    acc = own(xb4)

    recv(3)
    for g in range(blocks):
        out_ref[:, cells[g]] = (
            u_v[:, cells[g]] + (b_v[:, cells[g]] - (acc[g] + rest(xb4, g))) * scale[g]
        )
    for i in range(len(swaps)):
        sent(i)
    for copy in gathers:
        copy.wait_send()


def shards(
    right_side,
    start_field,
    fine_tiles,
    fine_links,
    fine_groups,
    mid_tiles,
    mid_links,
    mid_groups,
    last_inverse,
):
    sub = lax.axis_size("sub")
    n = lax.axis_size("rows") * sub
    blocks, _, tile, _ = fine_tiles.shape
    mid_blocks = mid_tiles.shape[0]
    rows = right_side.shape[0]
    last = last_inverse.shape[0]
    anywhere = pl.BlockSpec(memory_space=pl.ANY)
    scalars = pl.BlockSpec(memory_space=pltpu.SMEM)
    groups = fine_groups.reshape(blocks, tile)
    mid_groups = mid_groups.reshape(mid_blocks, tile)
    large = [right_side, start_field, fine_tiles, groups, mid_tiles, mid_groups, last_inverse]
    held = pltpu.VMEM((blocks + 2, rows, tile), BF16)
    return pl.pallas_call(
        functools.partial(kernel, n, sub),
        out_shape=jax.ShapeDtypeStruct(right_side.shape, F32),
        in_specs=[scalars] * 2 + [anywhere] * len(large),
        out_specs=pl.BlockSpec(memory_space=pltpu.VMEM),
        scratch_shapes=[pltpu.VMEM(x.shape, x.dtype) for x in large]
        + [held] * 5
        + [
            pltpu.VMEM((2, rows, tile), F32),
            pltpu.VMEM((2, rows, tile), F32),
            pltpu.VMEM((2, blocks, tile), jnp.int32),
            pltpu.VMEM((n, rows, tile), F32),
            pltpu.VMEM((tile, blocks * tile), BF16),
            pltpu.VMEM((mid_blocks, last, tile), BF16),
            pltpu.VMEM((mid_blocks, last, tile), BF16),
            pltpu.VMEM((mid_blocks, last, tile), BF16),
            pltpu.VMEM((mid_blocks, rows, tile), BF16),
            pltpu.VMEM((mid_blocks, rows, tile), F32),
            pltpu.SemaphoreType.DMA((len(large),)),
            pltpu.SemaphoreType.DMA((5, 2)),
            pltpu.SemaphoreType.DMA((5, 2)),
            pltpu.SemaphoreType.DMA((n - 1,)),
            pltpu.SemaphoreType.DMA((n - 1,)),
        ],
        compiler_params=pltpu.CompilerParams(
            collective_id=0, has_side_effects=True, vmem_limit_bytes=48 * 1024 * 1024
        ),
    )(fine_links, mid_links, *large)


def solution(mesh):
    in_specs = (
        P(("parts", "cols"), ("rows", "sub")),
        P(("parts", "cols"), ("rows", "sub")),
        P(("parts", "rows", "sub"), None, None, None),
        P(("parts", "rows", "sub"), None),
        P(("parts", "rows", "sub")),
        P("parts", None, None, None),
        P("parts", None),
        P("parts"),
        P("parts", None),
    )
    out_specs = P(("parts", "cols"), ("rows", "sub"))
    return jax.shard_map(shards, mesh=mesh, in_specs=in_specs, out_specs=out_specs, check_vma=False)
```

```python
import functools

import jax
import jax.numpy as jnp
from jax import lax
from jax.experimental import pallas as pl
from jax.experimental.pallas import tpu as pltpu
from jax.sharding import PartitionSpec as P

damping = 0.6
MESH = pl.DeviceIdType.MESH
F32 = jnp.float32
BF16 = jnp.bfloat16


def dot_nt(a, b):
    return lax.dot_general(a, b, (((1,), (1,)), ((), ())), preferred_element_type=F32)


def dot_nn(a, b):
    return lax.dot_general(a, b, (((1,), (0,)), ((), ())), preferred_element_type=F32)


def pieces(x, count):
    out = []
    for _ in range(count):
        high = x.astype(BF16)
        out.append(high)
        x = x - high.astype(F32)
    return jnp.concatenate(out, axis=0)


def unstack(y, count):
    rows = y.shape[0] // count
    total = y[(count - 1) * rows :]
    for i in range(count - 2, -1, -1):
        total = y[i * rows : (i + 1) * rows] + total
    return total


def one_hot_t(groups, base, rows, period):
    ids = lax.broadcasted_iota(jnp.int32, (rows, groups.shape[1]), 0)
    ids = lax.rem(ids, period) + base
    return jnp.where(ids == groups, 1.0, 0.0).astype(BF16)


def scale_of(tile):
    size = tile.shape[0]
    row = lax.broadcasted_iota(jnp.int32, (size, size), 0)
    col = lax.broadcasted_iota(jnp.int32, (size, size), 1)
    return damping / jnp.sum(jnp.where(row == col, tile.astype(F32), 0.0), axis=0, keepdims=True)


def kernel(
    n,
    sub,
    links,
    mid_links,
    b_any,
    u_any,
    t_any,
    grp_any,
    mt_any,
    mg_any,
    li_any,
    out_ref,
    b_v,
    u_v,
    t_v,
    grp_v,
    mt_v,
    mg_v,
    li_v,
    xb0,
    xb1,
    xb2,
    xb3,
    xb4,
    halo_f,
    ends_f,
    grp_h,
    slabs,
    own_pick,
    pt,
    ct,
    e_hi,
    e_lo,
    mb,
    mid_v,
    load_sem,
    halo_send,
    halo_recv,
    all_send,
    all_recv,
):
    blocks, tile = t_v.shape[0], t_v.shape[2]
    mid_blocks = mt_v.shape[0]
    last = li_v.shape[0]
    window = mid_blocks * tile // n
    assert 2 * window == tile
    me = lax.axis_index("rows") * sub + lax.axis_index("sub")
    has_left = me > 0
    has_right = me < n - 1

    def place(j):
        return {"rows": lax.div(j, sub), "sub": lax.rem(j, sub)}

    loads = [
        pltpu.make_async_copy(src, dst, load_sem.at[i])
        for i, (src, dst) in enumerate(
            (
                (u_any, u_v),
                (grp_any, grp_v),
                (t_any, t_v),
                (b_any, b_v),
                (mg_any, mg_v),
                (li_any, li_v),
                (mt_any, mt_v),
            )
        )
    ]
    for load in loads:
        load.start()

    barrier = pltpu.get_barrier_semaphore()
    for off in range(1, n):
        pl.semaphore_signal(
            barrier, inc=1, device_id=place(lax.rem(me + off, n)), device_id_type=MESH
        )

    left = jnp.maximum(me - 1, 0)
    right = jnp.minimum(me + 1, n - 1)

    def to_left(i, src, dst):
        return pltpu.make_async_remote_copy(
            src_ref=src,
            dst_ref=dst,
            send_sem=halo_send.at[i, 0],
            recv_sem=halo_recv.at[i, 1],
            device_id=place(left),
            device_id_type=MESH,
        )

    def to_right(i, src, dst):
        return pltpu.make_async_remote_copy(
            src_ref=src,
            dst_ref=dst,
            send_sem=halo_send.at[i, 1],
            recv_sem=halo_recv.at[i, 0],
            device_id=place(right),
            device_id_type=MESH,
        )

    def pair(i, first, final, before, after):
        return to_left(i, first, after), to_right(i, final, before)

    def ends(i, xb):
        return pair(i, xb.at[1], xb.at[blocks], xb.at[0], xb.at[blocks + 1])

    swaps = [
        ends(0, xb0),
        ends(1, xb1),
        pair(2, ends_f.at[0], ends_f.at[1], halo_f.at[0], halo_f.at[1]),
        ends(3, xb4),
        pair(4, grp_v, grp_v, grp_h.at[0], grp_h.at[1]),
    ]

    def send(i):
        @pl.when(has_left)
        def _():
            swaps[i][0].start()

        @pl.when(has_right)
        def _():
            swaps[i][1].start()

    def recv(i):
        @pl.when(has_left)
        def _():
            swaps[i][1].wait_recv()

        @pl.when(has_right)
        def _():
            swaps[i][0].wait_recv()

    def sent(i):
        @pl.when(has_left)
        def _():
            swaps[i][0].wait_send()

        @pl.when(has_right)
        def _():
            swaps[i][1].wait_send()

    zero_b = jnp.zeros(xb0.shape[1:], BF16)
    zero_f = jnp.zeros(halo_f.shape[1:], F32)

    @pl.when(me == 0)
    def _():
        for xb in (xb0, xb1, xb4):
            xb[0] = zero_b
        halo_f[0] = zero_f
        grp_h[0] = jnp.zeros(grp_h.shape[1:], jnp.int32)

    @pl.when(me == n - 1)
    def _():
        for xb in (xb0, xb1, xb4):
            xb[blocks + 1] = zero_b
        halo_f[1] = zero_f
        grp_h[1] = jnp.zeros(grp_h.shape[1:], jnp.int32)

    order = [0, blocks - 1] + list(range(1, blocks - 1))
    cells = [slice(g * tile, (g + 1) * tile) for g in range(blocks)]

    loads[0].wait()
    for g in order:
        xb0[g + 1] = u_v[:, cells[g]].astype(BF16)
    loads[1].wait()
    pl.semaphore_wait(barrier, n - 1)
    send(0)
    send(4)

    def own(xb):
        return [dot_nt(xb[g + 1], t_v[g, 0]) for g in range(blocks)]

    def rest(xb, g):
        picked = jnp.concatenate([xb[links[1, g]], xb[links[2, g]]], axis=1)
        return dot_nt(picked, jnp.concatenate([t_v[g, 1], t_v[g, 2]], axis=1))

    loads[2].wait()
    loads[3].wait()
    acc = own(xb0)
    scale = [scale_of(t_v[g, 0]) for g in range(blocks)]

    recv(0)
    for g in order:
        new = u_v[:, cells[g]] + (b_v[:, cells[g]] - (acc[g] + rest(xb0, g))) * scale[g]
        u_v[:, cells[g]] = new
        xb1[g + 1] = new.astype(BF16)
        if g == blocks - 1:
            send(1)
    acc = own(xb1)

    for g in range(blocks):
        own_pick[:, cells[g]] = one_hot_t(grp_v[g : g + 1], me * window, tile, window)

    recv(1)
    for g in order:
        new = u_v[:, cells[g]] + (b_v[:, cells[g]] - (acc[g] + rest(xb1, g))) * scale[g]
        u_v[:, cells[g]] = new
        xb2[g + 1] = new.astype(BF16)
        if g == 0:
            ends_f[0] = new
        if g == blocks - 1:
            ends_f[1] = new
            send(2)
    acc = own(xb2)

    recv(2)
    xb2[0] = halo_f[0].astype(BF16)
    xb2[blocks + 1] = halo_f[1].astype(BF16)
    resid = jnp.concatenate(
        [pieces(b_v[:, cells[g]] - (acc[g] + rest(xb2, g)), 3) for g in range(blocks)], axis=1
    )
    sums = unstack(dot_nt(resid, own_pick[...]), 3)
    half = sums.shape[0] // 2
    low = lax.broadcasted_iota(jnp.int32, (half, tile), 1) < window
    odd = lax.rem(me, 2) == 1
    slabs[me] = jnp.where(jnp.logical_xor(low, odd), sums[:half], sums[half:])
    gathers = []
    for off in range(n - 1, 0, -1):
        copy = pltpu.make_async_remote_copy(
            src_ref=slabs.at[me],
            dst_ref=slabs.at[me],
            send_sem=all_send.at[off - 1],
            recv_sem=all_recv.at[off - 1],
            device_id=place(lax.rem(me + off, n)),
            device_id_type=MESH,
        )
        copy.start()
        gathers.append(copy)

    for i in (4, 5, 6):
        loads[i].wait()
    flipped = li_v[...].T
    flipped_hi = flipped.astype(BF16)
    flipped_lo = (flipped - flipped_hi.astype(F32)).astype(BF16)
    for m in range(mid_blocks):
        hot = one_hot_t(mg_v[m : m + 1], 0, last, last)
        ct[m] = hot
        e_hi[m] = dot_nn(flipped_hi, hot).astype(BF16)
        e_lo[m] = dot_nn(flipped_lo, hot).astype(BF16)
    mid_scale = [scale_of(mt_v[m, 0]) for m in range(mid_blocks)]
    for g in range(blocks):
        pt[:, cells[g]] = one_hot_t(grp_v[g : g + 1], lax.div(me, 2) * tile, tile, tile)
    recv(4)
    hot_left = one_hot_t(grp_h[0, blocks - 1 : blocks], lax.div(left, 2) * tile, tile, tile)
    hot_right = one_hot_t(grp_h[1, 0:1], lax.div(right, 2) * tile, tile, tile)
    for copy in gathers:
        copy.wait_recv()

    side = []
    for m in range(mid_blocks):
        even, other = slabs[2 * m], slabs[2 * m + 1]
        top = jnp.where(low, even, other)
        bottom = pltpu.roll(jnp.where(low, other, even), window, 1)
        side.append(jnp.concatenate([top, bottom], axis=0))

    def mid_apply(values):
        for m in range(mid_blocks):
            mb[m] = values[m].astype(BF16)
        out = []
        for m in range(mid_blocks):
            picked = jnp.concatenate(
                [mb[m], mb[mid_links[m, 1]], mb[mid_links[m, 2]]], axis=1
            )
            out.append(
                dot_nt(picked, jnp.concatenate([mt_v[m, 0], mt_v[m, 1], mt_v[m, 2]], axis=1))
            )
        return out

    def mid_sweep(values):
        return [
            v + (s - a) * d for v, s, a, d in zip(values, side, mid_apply(values), mid_scale)
        ]

    mid = [s * d for s, d in zip(side, mid_scale)]
    mid = mid_sweep(mid)
    mid_resid = [s - a for s, a in zip(side, mid_apply(mid))]
    last_side = dot_nt(pieces(mid_resid[0], 2), ct[0])
    for m in range(1, mid_blocks):
        last_side = last_side + dot_nt(pieces(mid_resid[m], 2), ct[m])
    both = pieces(unstack(last_side, 2), 2)
    high = both[: both.shape[0] // 2]
    mid = [
        mid[m] + (unstack(dot_nn(both, e_hi[m]), 2) + dot_nn(high, e_lo[m]))
        for m in range(mid_blocks)
    ]
    mid = mid_sweep(mid)
    mid = mid_sweep(mid)
    for m in range(mid_blocks):
        mid_v[m] = mid[m]

    def lift(device, hot):
        return unstack(dot_nn(pieces(mid_v[lax.div(device, 2)], 3), hot), 3)

    add = lift(me, pt[...])
    before = halo_f[0] + lift(left, hot_left)
    after = halo_f[1] + lift(right, hot_right)
    xb3[0] = jnp.where(has_left, before, 0.0).astype(BF16)
    xb3[blocks + 1] = jnp.where(has_right, after, 0.0).astype(BF16)
    for g in range(blocks):
        new = u_v[:, cells[g]] + add[:, cells[g]]
        u_v[:, cells[g]] = new
        xb3[g + 1] = new.astype(BF16)

    acc = own(xb3)
    for g in order:
        new = u_v[:, cells[g]] + (b_v[:, cells[g]] - (acc[g] + rest(xb3, g))) * scale[g]
        u_v[:, cells[g]] = new
        xb4[g + 1] = new.astype(BF16)
        if g == blocks - 1:
            send(3)
    acc = own(xb4)

    recv(3)
    for g in range(blocks):
        out_ref[:, cells[g]] = (
            u_v[:, cells[g]] + (b_v[:, cells[g]] - (acc[g] + rest(xb4, g))) * scale[g]
        )
    for i in range(len(swaps)):
        sent(i)
    for copy in gathers:
        copy.wait_send()


def shards(
    right_side,
    start_field,
    fine_tiles,
    fine_links,
    fine_groups,
    mid_tiles,
    mid_links,
    mid_groups,
    last_inverse,
):
    sub = lax.axis_size("sub")
    n = lax.axis_size("rows") * sub
    blocks, _, tile, _ = fine_tiles.shape
    mid_blocks = mid_tiles.shape[0]
    rows = right_side.shape[0]
    last = last_inverse.shape[0]
    anywhere = pl.BlockSpec(memory_space=pltpu.HBM)
    scalars = pl.BlockSpec(memory_space=pltpu.SMEM)
    groups = fine_groups.reshape(blocks, tile)
    mid_groups = mid_groups.reshape(mid_blocks, tile)
    large = [right_side, start_field, fine_tiles, groups, mid_tiles, mid_groups, last_inverse]
    held = pltpu.VMEM((blocks + 2, rows, tile), BF16)
    return pl.pallas_call(
        functools.partial(kernel, n, sub),
        out_shape=jax.ShapeDtypeStruct(right_side.shape, F32),
        in_specs=[scalars] * 2 + [anywhere] * len(large),
        out_specs=pl.BlockSpec(memory_space=pltpu.VMEM),
        scratch_shapes=[pltpu.VMEM(x.shape, x.dtype) for x in large]
        + [held] * 5
        + [
            pltpu.VMEM((2, rows, tile), F32),
            pltpu.VMEM((2, rows, tile), F32),
            pltpu.VMEM((2, blocks, tile), jnp.int32),
            pltpu.VMEM((n, rows // 2, tile), F32),
            pltpu.VMEM((tile, blocks * tile), BF16),
            pltpu.VMEM((tile, blocks * tile), BF16),
            pltpu.VMEM((mid_blocks, last, tile), BF16),
            pltpu.VMEM((mid_blocks, last, tile), BF16),
            pltpu.VMEM((mid_blocks, last, tile), BF16),
            pltpu.VMEM((mid_blocks, rows, tile), BF16),
            pltpu.VMEM((mid_blocks, rows, tile), F32),
            pltpu.SemaphoreType.DMA((len(large),)),
            pltpu.SemaphoreType.DMA((5, 2)),
            pltpu.SemaphoreType.DMA((5, 2)),
            pltpu.SemaphoreType.DMA((n - 1,)),
            pltpu.SemaphoreType.DMA((n - 1,)),
        ],
        compiler_params=pltpu.CompilerParams(
            collective_id=0, has_side_effects=True, vmem_limit_bytes=60 * 1024 * 1024
        ),
    )(fine_links.T, mid_links, *large)


def solution(mesh):
    in_specs = (
        P(("parts", "cols"), ("rows", "sub")),
        P(("parts", "cols"), ("rows", "sub")),
        P(("parts", "rows", "sub"), None, None, None),
        P(("parts", "rows", "sub"), None),
        P(("parts", "rows", "sub")),
        P("parts", None, None, None),
        P("parts", None),
        P("parts"),
        P("parts", None),
    )
    out_specs = P(("parts", "cols"), ("rows", "sub"))
    return jax.shard_map(shards, mesh=mesh, in_specs=in_specs, out_specs=out_specs, check_vma=False)
```

```python
import functools

import jax
import jax.numpy as jnp
from jax import lax
from jax.experimental import pallas as pl
from jax.experimental.pallas import tpu as pltpu
from jax.sharding import PartitionSpec as P

damping = 0.6
MESH = pl.DeviceIdType.MESH
F32 = jnp.float32
BF16 = jnp.bfloat16


def dot_nt(a, b):
    return lax.dot_general(a, b, (((1,), (1,)), ((), ())), preferred_element_type=F32)


def dot_nn(a, b):
    return lax.dot_general(a, b, (((1,), (0,)), ((), ())), preferred_element_type=F32)


def pieces(x, count):
    out = []
    for _ in range(count):
        high = x.astype(BF16)
        out.append(high)
        x = x - high.astype(F32)
    return jnp.concatenate(out, axis=0)


def unstack(y, count):
    rows = y.shape[0] // count
    total = y[(count - 1) * rows :]
    for i in range(count - 2, -1, -1):
        total = y[i * rows : (i + 1) * rows] + total
    return total


def one_hot_t(groups, base, rows, period):
    ids = lax.broadcasted_iota(jnp.int32, (rows, groups.shape[1]), 0)
    ids = lax.rem(ids, period) + base
    return jnp.where(ids == groups, 1.0, 0.0).astype(BF16)


def scale_of(tile):
    size = tile.shape[0]
    row = lax.broadcasted_iota(jnp.int32, (size, size), 0)
    col = lax.broadcasted_iota(jnp.int32, (size, size), 1)
    return damping / jnp.sum(jnp.where(row == col, tile.astype(F32), 0.0), axis=0, keepdims=True)


def kernel(
    n,
    sub,
    links,
    mid_links,
    b_any,
    u_any,
    t_any,
    grp_any,
    mt_any,
    mg_any,
    li_any,
    out_ref,
    b_v,
    u_v,
    t_v,
    grp_v,
    mt_v,
    mg_v,
    li_v,
    xb0,
    xb1,
    xb2,
    xb3,
    xb4,
    meta_v,
    meta_h,
    meta_f,
    tiles_h,
    b_h,
    u1_e,
    u1_h,
    pick1,
    pick1_h,
    far1_h,
    u2,
    u2_h,
    pick2,
    pick2_h,
    far2_h,
    slabs,
    own_pick,
    pt,
    ct,
    e_hi,
    e_lo,
    mb,
    mid_v,
    load_sem,
    halo_send,
    halo_recv,
    all_send,
    all_recv,
):
    blocks, tile = t_v.shape[0], t_v.shape[2]
    mid_blocks = mt_v.shape[0]
    last = li_v.shape[0]
    window = mid_blocks * tile // n
    assert 2 * window == tile
    me = lax.axis_index("rows") * sub + lax.axis_index("sub")
    has_left = me > 0
    has_right = me < n - 1

    def place(j):
        return {"rows": lax.div(j, sub), "sub": lax.rem(j, sub)}

    loads = [
        pltpu.make_async_copy(src, dst, load_sem.at[i])
        for i, (src, dst) in enumerate(
            (
                (u_any, u_v),
                (grp_any, grp_v),
                (t_any, t_v),
                (b_any, b_v),
                (mg_any, mg_v),
                (li_any, li_v),
                (mt_any, mt_v),
            )
        )
    ]
    for load in loads:
        load.start()

    barrier = pltpu.get_barrier_semaphore()
    for off in range(1, n):
        pl.semaphore_signal(
            barrier, inc=1, device_id=place(lax.rem(me + off, n)), device_id_type=MESH
        )

    left, left2 = jnp.maximum(me - 1, 0), jnp.maximum(me - 2, 0)
    right, right2 = jnp.minimum(me + 1, n - 1), jnp.minimum(me + 2, n - 1)

    def pair(i, first, final, arrived, far=False):
        def copy(src, side, device):
            return pltpu.make_async_remote_copy(
                src_ref=src,
                dst_ref=arrived[1 - side],
                send_sem=halo_send.at[i, side],
                recv_sem=halo_recv.at[i, 1 - side],
                device_id=place(device),
                device_id_type=MESH,
            )

        to_left = copy(first, 0, left2 if far else left)
        to_right = copy(final, 1, right2 if far else right)
        return to_left, to_right, (me > 1 if far else has_left), (me < n - 2 if far else has_right)

    def sides(ref):
        return ref.at[0], ref.at[1]

    edge = slice(0, tile), slice((blocks - 1) * tile, blocks * tile)
    swaps = [
        pair(0, xb0.at[1], xb0.at[blocks], (xb0.at[0], xb0.at[blocks + 1])),
        pair(1, meta_v, meta_v, sides(meta_h)),
        pair(2, t_v.at[0], t_v.at[blocks - 1], sides(tiles_h)),
        pair(3, b_v.at[:, edge[0]], b_v.at[:, edge[1]], sides(b_h)),
        pair(4, u1_e.at[0], u1_e.at[1], sides(u1_h)),
        pair(5, pick1.at[0], pick1.at[1], sides(pick1_h)),
        pair(6, xb1.at[1], xb1.at[blocks], sides(far1_h), far=True),
        pair(7, meta_v, meta_v, sides(meta_f), far=True),
        pair(8, pick2.at[0], pick2.at[1], sides(pick2_h)),
        pair(9, u2.at[0], u2.at[blocks - 1], sides(far2_h), far=True),
    ]

    def send(i):
        to_left, to_right, some_left, some_right = swaps[i]

        @pl.when(some_left)
        def _():
            to_left.start()

        @pl.when(some_right)
        def _():
            to_right.start()

    def recv(i):
        to_left, to_right, some_left, some_right = swaps[i]

        @pl.when(some_left)
        def _():
            to_right.wait_recv()

        @pl.when(some_right)
        def _():
            to_left.wait_recv()

    def sent(i):
        to_left, to_right, some_left, some_right = swaps[i]

        @pl.when(some_left)
        def _():
            to_left.wait_send()

        @pl.when(some_right)
        def _():
            to_right.wait_send()

    def clear(ref, i):
        ref[i] = jnp.zeros(ref.shape[1:], ref.dtype)

    for i in (0, blocks + 1):
        clear(xb1, i)
    for side, near_edge, far_edge in (
        (0, me == 0, me <= 1),
        (1, me == n - 1, me >= n - 2),
    ):

        @pl.when(near_edge)
        def _():
            clear(xb0, side * (blocks + 1))
            for ref in (meta_h, tiles_h, b_h, u1_h, pick1_h, pick2_h):
                clear(ref, side)

        @pl.when(far_edge)
        def _():
            for ref in (meta_f, far1_h, far2_h):
                clear(ref, side)

    order = [0, blocks - 1] + list(range(1, blocks - 1))
    cells = [slice(g * tile, (g + 1) * tile) for g in range(blocks)]

    loads[0].wait()
    for g in order:
        xb0[g + 1] = u_v[:, cells[g]].astype(BF16)
    loads[1].wait()
    pl.semaphore_wait(barrier, n - 1)
    send(0)
    outer = links[2, 0], links[1, blocks - 1]
    inner = [jnp.clip(link - 1, 0, blocks - 1) for link in outer]
    meta_v[...] = jnp.zeros(meta_v.shape, jnp.int32)
    meta_v[0:blocks] = grp_v[...]
    for side in (0, 1):
        meta_v[blocks + side : blocks + side + 1] = jnp.full((1, tile), outer[side], jnp.int32)
        meta_v[blocks + 2 + side : blocks + 3 + side] = grp_v[pl.ds(inner[side], 1)]
    send(1)
    send(7)

    def own(xb):
        return [dot_nt(xb[g + 1], t_v[g, 0]) for g in range(blocks)]

    def rest(xb, g):
        picked = jnp.concatenate([xb[links[1, g]], xb[links[2, g]]], axis=1)
        return dot_nt(picked, jnp.concatenate([t_v[g, 1], t_v[g, 2]], axis=1))

    loads[2].wait()
    send(2)
    loads[3].wait()
    send(3)
    acc = own(xb0)
    scale = [scale_of(t_v[g, 0]) for g in range(blocks)]

    recv(0)
    for g in order:
        new = u_v[:, cells[g]] + (b_v[:, cells[g]] - (acc[g] + rest(xb0, g))) * scale[g]
        u_v[:, cells[g]] = new
        xb1[g + 1] = new.astype(BF16)
        if g == 0:
            u1_e[0] = new
        if g == blocks - 1:
            u1_e[1] = new
            send(6)
            send(4)
    for side in (0, 1):
        pick1[side] = xb1[inner[side] + 1]
    send(5)
    acc = own(xb1)

    for g in range(blocks):
        own_pick[:, cells[g]] = one_hot_t(grp_v[g : g + 1], me * window, tile, window)

    def select(side, own, far, near):
        link = meta_h[side, blocks + 1 - side : blocks + 2 - side]
        mine, beyond = (blocks + 1, 0) if side == 0 else (0, blocks + 1)
        return jnp.where(link == mine, own, jnp.where(link == beyond, far, near))

    def follow(side, xb, field, far, near):
        end, own = xb[side * (blocks + 1)], xb[1 if side == 0 else blocks]
        other = select(side, own.astype(F32), far, near).astype(BF16)
        parts = [end, other, own] if side == 0 else [end, own, other]
        product = dot_nt(
            jnp.concatenate(parts, axis=1),
            jnp.concatenate([tiles_h[side, k] for k in range(3)], axis=1),
        )
        new = field + (b_h[side] - product) * scale_of(tiles_h[side, 0])
        return jnp.where(has_right if side else has_left, new, 0.0)

    for i in (1, 2, 3, 4, 5, 6):
        recv(i)
    for side in (0, 1):
        xb1[side * (blocks + 1)] = u1_h[side].astype(BF16)
    for side in (0, 1):
        new = follow(
            side, xb1, u1_h[side], far1_h[side].astype(F32), pick1_h[side].astype(F32)
        )
        u2_h[side] = new
        xb2[side * (blocks + 1)] = new.astype(BF16)
    for g in order:
        new = u_v[:, cells[g]] + (b_v[:, cells[g]] - (acc[g] + rest(xb1, g))) * scale[g]
        u_v[:, cells[g]] = new
        u2[g] = new
        xb2[g + 1] = new.astype(BF16)
    acc = own(xb2)

    resid = jnp.concatenate(
        [pieces(b_v[:, cells[g]] - (acc[g] + rest(xb2, g)), 3) for g in range(blocks)], axis=1
    )
    sums = unstack(dot_nt(resid, own_pick[...]), 3)
    half = sums.shape[0] // 2
    low = lax.broadcasted_iota(jnp.int32, (half, tile), 1) < window
    odd = lax.rem(me, 2) == 1
    slabs[me] = jnp.where(jnp.logical_xor(low, odd), sums[:half], sums[half:])
    gathers = []
    for off in range(n - 1, 0, -1):
        copy = pltpu.make_async_remote_copy(
            src_ref=slabs.at[me],
            dst_ref=slabs.at[me],
            send_sem=all_send.at[off - 1],
            recv_sem=all_recv.at[off - 1],
            device_id=place(lax.rem(me + off, n)),
            device_id_type=MESH,
        )
        copy.start()
        gathers.append(copy)
    for side in (0, 1):
        pick2[side] = u2[inner[side]]
    send(8)
    send(9)

    for i in (4, 5, 6):
        loads[i].wait()
    flipped = li_v[...].T
    flipped_hi = flipped.astype(BF16)
    flipped_lo = (flipped - flipped_hi.astype(F32)).astype(BF16)
    for m in range(mid_blocks):
        hot = one_hot_t(mg_v[m : m + 1], 0, last, last)
        ct[m] = hot
        e_hi[m] = dot_nn(flipped_hi, hot).astype(BF16)
        e_lo[m] = dot_nn(flipped_lo, hot).astype(BF16)
    mid_scale = [scale_of(mt_v[m, 0]) for m in range(mid_blocks)]
    for g in range(blocks):
        pt[:, cells[g]] = one_hot_t(grp_v[g : g + 1], lax.div(me, 2) * tile, tile, tile)
    recv(7)

    def hot(meta, device):
        return one_hot_t(meta, lax.div(device, 2) * tile, tile, tile)

    beside = ((left, left2, blocks - 1), (right, right2, 0))
    hots = [
        (
            hot(meta_h[side, row : row + 1], near),
            hot(meta_h[side, blocks + 3 - side : blocks + 4 - side], near),
            hot(meta_f[side, row : row + 1], far),
        )
        for side, (near, far, row) in enumerate(beside)
    ]
    for copy in gathers:
        copy.wait_recv()

    side = []
    for m in range(mid_blocks):
        even, other = slabs[2 * m], slabs[2 * m + 1]
        top = jnp.where(low, even, other)
        bottom = pltpu.roll(jnp.where(low, other, even), window, 1)
        side.append(jnp.concatenate([top, bottom], axis=0))

    def mid_apply(values):
        for m in range(mid_blocks):
            mb[m] = values[m].astype(BF16)
        out = []
        for m in range(mid_blocks):
            picked = jnp.concatenate(
                [mb[m], mb[mid_links[m, 1]], mb[mid_links[m, 2]]], axis=1
            )
            out.append(
                dot_nt(picked, jnp.concatenate([mt_v[m, 0], mt_v[m, 1], mt_v[m, 2]], axis=1))
            )
        return out

    def mid_sweep(values):
        return [
            v + (s - a) * d for v, s, a, d in zip(values, side, mid_apply(values), mid_scale)
        ]

    mid = [s * d for s, d in zip(side, mid_scale)]
    mid = mid_sweep(mid)
    mid_resid = [s - a for s, a in zip(side, mid_apply(mid))]
    last_side = dot_nt(pieces(mid_resid[0], 2), ct[0])
    for m in range(1, mid_blocks):
        last_side = last_side + dot_nt(pieces(mid_resid[m], 2), ct[m])
    both = pieces(unstack(last_side, 2), 2)
    high = both[: both.shape[0] // 2]
    mid = [
        mid[m] + (unstack(dot_nn(both, e_hi[m]), 2) + dot_nn(high, e_lo[m]))
        for m in range(mid_blocks)
    ]
    mid = mid_sweep(mid)
    mid = mid_sweep(mid)
    for m in range(mid_blocks):
        mid_v[m] = mid[m]

    def lift(device, hot):
        return unstack(dot_nn(pieces(mid_v[lax.div(device, 2)], 3), hot), 3)

    add = lift(me, pt[...])
    recv(8)
    recv(9)
    u3_h = []
    for side, (near, far, _) in enumerate(beside):
        end = u2_h[side] + lift(near, hots[side][0])
        end = jnp.where(has_right if side else has_left, end, 0.0)
        xb3[side * (blocks + 1)] = end.astype(BF16)
        picked = pick2_h[side] + lift(near, hots[side][1])
        beyond = far2_h[side] + lift(far, hots[side][2])
        beyond = jnp.where(me < n - 2 if side else me > 1, beyond, 0.0)
        u3_h.append((end, beyond, picked))
    for g in range(blocks):
        new = u_v[:, cells[g]] + add[:, cells[g]]
        u_v[:, cells[g]] = new
        xb3[g + 1] = new.astype(BF16)

    acc = own(xb3)
    for side in (0, 1):
        xb4[side * (blocks + 1)] = follow(side, xb3, *u3_h[side]).astype(BF16)
    for g in order:
        new = u_v[:, cells[g]] + (b_v[:, cells[g]] - (acc[g] + rest(xb3, g))) * scale[g]
        u_v[:, cells[g]] = new
        xb4[g + 1] = new.astype(BF16)
    acc = own(xb4)

    for g in range(blocks):
        out_ref[:, cells[g]] = (
            u_v[:, cells[g]] + (b_v[:, cells[g]] - (acc[g] + rest(xb4, g))) * scale[g]
        )
    for i in range(len(swaps)):
        sent(i)
    for copy in gathers:
        copy.wait_send()


def shards(
    right_side,
    start_field,
    fine_tiles,
    fine_links,
    fine_groups,
    mid_tiles,
    mid_links,
    mid_groups,
    last_inverse,
):
    sub = lax.axis_size("sub")
    n = lax.axis_size("rows") * sub
    blocks, _, tile, _ = fine_tiles.shape
    mid_blocks = mid_tiles.shape[0]
    rows = right_side.shape[0]
    last = last_inverse.shape[0]
    anywhere = pl.BlockSpec(memory_space=pltpu.HBM)
    scalars = pl.BlockSpec(memory_space=pltpu.SMEM)
    groups = fine_groups.reshape(blocks, tile)
    mid_groups = mid_groups.reshape(mid_blocks, tile)
    large = [right_side, start_field, fine_tiles, groups, mid_tiles, mid_groups, last_inverse]
    held = pltpu.VMEM((blocks + 2, rows, tile), BF16)
    return pl.pallas_call(
        functools.partial(kernel, n, sub),
        out_shape=jax.ShapeDtypeStruct(right_side.shape, F32),
        in_specs=[scalars] * 2 + [anywhere] * len(large),
        out_specs=pl.BlockSpec(memory_space=pltpu.VMEM),
        scratch_shapes=[pltpu.VMEM(x.shape, x.dtype) for x in large]
        + [held] * 5
        + [
            pltpu.VMEM((blocks + 8, tile), jnp.int32),
            pltpu.VMEM((2, blocks + 8, tile), jnp.int32),
            pltpu.VMEM((2, blocks + 8, tile), jnp.int32),
            pltpu.VMEM((2,) + fine_tiles.shape[1:], BF16),
            pltpu.VMEM((2, rows, tile), F32),
            pltpu.VMEM((2, rows, tile), F32),
            pltpu.VMEM((2, rows, tile), F32),
            pltpu.VMEM((2, rows, tile), BF16),
            pltpu.VMEM((2, rows, tile), BF16),
            pltpu.VMEM((2, rows, tile), BF16),
            pltpu.VMEM((blocks, rows, tile), F32),
            pltpu.VMEM((2, rows, tile), F32),
            pltpu.VMEM((2, rows, tile), F32),
            pltpu.VMEM((2, rows, tile), F32),
            pltpu.VMEM((2, rows, tile), F32),
            pltpu.VMEM((n, rows // 2, tile), F32),
            pltpu.VMEM((tile, blocks * tile), BF16),
            pltpu.VMEM((tile, blocks * tile), BF16),
            pltpu.VMEM((mid_blocks, last, tile), BF16),
            pltpu.VMEM((mid_blocks, last, tile), BF16),
            pltpu.VMEM((mid_blocks, last, tile), BF16),
            pltpu.VMEM((mid_blocks, rows, tile), BF16),
            pltpu.VMEM((mid_blocks, rows, tile), F32),
            pltpu.SemaphoreType.DMA((len(large),)),
            pltpu.SemaphoreType.DMA((10, 2)),
            pltpu.SemaphoreType.DMA((10, 2)),
            pltpu.SemaphoreType.DMA((n - 1,)),
            pltpu.SemaphoreType.DMA((n - 1,)),
        ],
        compiler_params=pltpu.CompilerParams(
            collective_id=0, has_side_effects=True, vmem_limit_bytes=56308531
        ),
    )(fine_links.T, mid_links, *large)


def solution(mesh):
    in_specs = (
        P(("parts", "cols"), ("rows", "sub")),
        P(("parts", "cols"), ("rows", "sub")),
        P(("parts", "rows", "sub"), None, None, None),
        P(("parts", "rows", "sub"), None),
        P(("parts", "rows", "sub")),
        P("parts", None, None, None),
        P("parts", None),
        P("parts"),
        P("parts", None),
    )
    out_specs = P(("parts", "cols"), ("rows", "sub"))
    return jax.shard_map(shards, mesh=mesh, in_specs=in_specs, out_specs=out_specs, check_vma=False)
```

```python
import functools

import jax
import jax.numpy as jnp
from jax import lax
from jax.experimental import pallas as pl
from jax.experimental.pallas import tpu as pltpu
from jax.sharding import PartitionSpec as P

damping = 0.6
MESH = pl.DeviceIdType.MESH
F32 = jnp.float32
BF16 = jnp.bfloat16


def dot_nt(a, b):
    return lax.dot_general(a, b, (((1,), (1,)), ((), ())), preferred_element_type=F32)


def dot_nn(a, b):
    return lax.dot_general(a, b, (((1,), (0,)), ((), ())), preferred_element_type=F32)


def pieces(x, count):
    out = []
    for _ in range(count):
        high = x.astype(BF16)
        out.append(high)
        x = x - high.astype(F32)
    return jnp.concatenate(out, axis=0)


def unstack(y, count):
    rows = y.shape[0] // count
    total = y[(count - 1) * rows :]
    for i in range(count - 2, -1, -1):
        total = y[i * rows : (i + 1) * rows] + total
    return total


def one_hot_t(groups, base, rows, period):
    ids = lax.broadcasted_iota(jnp.int32, (rows, groups.shape[1]), 0)
    ids = lax.rem(ids, period) + base
    return jnp.where(ids == groups, 1.0, 0.0).astype(BF16)


def scale_of(tile):
    size = tile.shape[0]
    row = lax.broadcasted_iota(jnp.int32, (size, size), 0)
    col = lax.broadcasted_iota(jnp.int32, (size, size), 1)
    return damping / jnp.sum(jnp.where(row == col, tile.astype(F32), 0.0), axis=0, keepdims=True)


def kernel(
    n,
    sub,
    links,
    mid_links,
    b_any,
    u_any,
    t_any,
    grp_any,
    mt_any,
    mg_any,
    li_any,
    out_ref,
    b_v,
    u_v,
    t_v,
    grp_v,
    mt_v,
    mg_v,
    li_v,
    xb0,
    xb1,
    xb2,
    xb3,
    xb4,
    meta_v,
    meta_h,
    meta_f,
    tiles_h,
    b_h,
    u1_e,
    u1_h,
    pick1,
    pick1_h,
    far1_h,
    u2,
    u2_h,
    pick2,
    pick2_h,
    far2_h,
    slabs,
    own_pick,
    pt,
    ct,
    e_hi,
    e_lo,
    mb,
    mid_v,
    load_sem,
    halo_send,
    halo_recv,
    all_send,
    all_recv,
    round_sem,
):
    blocks, tile = t_v.shape[0], t_v.shape[2]
    mid_blocks = mt_v.shape[0]
    last = li_v.shape[0]
    window = mid_blocks * tile // n
    assert 2 * window == tile
    me = lax.axis_index("rows") * sub + lax.axis_index("sub")
    has_left = me > 0
    has_right = me < n - 1

    def place(j):
        return {"rows": lax.div(j, sub), "sub": lax.rem(j, sub)}

    loads = [
        pltpu.make_async_copy(src, dst, load_sem.at[i])
        for i, (src, dst) in enumerate(
            (
                (u_any, u_v),
                (grp_any, grp_v),
                (t_any, t_v),
                (b_any, b_v),
                (mg_any, mg_v),
                (li_any, li_v),
                (mt_any, mt_v),
            )
        )
    ]
    for load in loads:
        load.start()

    def greet(sem, distance):
        for there in (me - distance, me + distance):

            @pl.when(jnp.logical_and(there >= 0, there < n))
            def _():
                pl.semaphore_signal(sem, inc=1, device_id=place(there), device_id_type=MESH)

    def greeted(sem, *distances):
        count = jnp.int32(0)
        for distance in distances:
            count = count + jnp.where(me >= distance, 1, 0) + jnp.where(me + distance < n, 1, 0)
        pl.semaphore_wait(sem, count)

    barrier = pltpu.get_barrier_semaphore()
    for distance in (1, 2):
        greet(barrier, distance)
    reaches = [2]
    while 2 * reaches[-1] < n - 1:
        reaches.append(2 * reaches[-1])

    left, left2 = jnp.maximum(me - 1, 0), jnp.maximum(me - 2, 0)
    right, right2 = jnp.minimum(me + 1, n - 1), jnp.minimum(me + 2, n - 1)

    def pair(i, first, final, arrived, far=False):
        def copy(src, side, device):
            return pltpu.make_async_remote_copy(
                src_ref=src,
                dst_ref=arrived[1 - side],
                send_sem=halo_send.at[i, side],
                recv_sem=halo_recv.at[i, 1 - side],
                device_id=place(device),
                device_id_type=MESH,
            )

        to_left = copy(first, 0, left2 if far else left)
        to_right = copy(final, 1, right2 if far else right)
        return to_left, to_right, (me > 1 if far else has_left), (me < n - 2 if far else has_right)

    def sides(ref):
        return ref.at[0], ref.at[1]

    edge = slice(0, tile), slice((blocks - 1) * tile, blocks * tile)
    swaps = [
        pair(0, xb0.at[1], xb0.at[blocks], (xb0.at[0], xb0.at[blocks + 1])),
        pair(1, meta_v, meta_v, sides(meta_h)),
        pair(2, t_v.at[0], t_v.at[blocks - 1], sides(tiles_h)),
        pair(3, b_v.at[:, edge[0]], b_v.at[:, edge[1]], sides(b_h)),
        pair(4, u1_e.at[0], u1_e.at[1], sides(u1_h)),
        pair(5, pick1.at[0], pick1.at[1], sides(pick1_h)),
        pair(6, xb1.at[1], xb1.at[blocks], sides(far1_h), far=True),
        pair(7, meta_v, meta_v, sides(meta_f), far=True),
        pair(8, pick2.at[0], pick2.at[1], sides(pick2_h)),
        pair(9, u2.at[0], u2.at[blocks - 1], sides(far2_h), far=True),
    ]

    def send(i):
        to_left, to_right, some_left, some_right = swaps[i]

        @pl.when(some_left)
        def _():
            to_left.start()

        @pl.when(some_right)
        def _():
            to_right.start()

    def recv(i):
        to_left, to_right, some_left, some_right = swaps[i]

        @pl.when(some_left)
        def _():
            to_right.wait_recv()

        @pl.when(some_right)
        def _():
            to_left.wait_recv()

    def sent(i):
        to_left, to_right, some_left, some_right = swaps[i]

        @pl.when(some_left)
        def _():
            to_left.wait_send()

        @pl.when(some_right)
        def _():
            to_right.wait_send()

    def clear(ref, i):
        ref[i] = jnp.zeros(ref.shape[1:], ref.dtype)

    for i in (0, blocks + 1):
        clear(xb1, i)
    for side, near_edge, far_edge in (
        (0, me == 0, me <= 1),
        (1, me == n - 1, me >= n - 2),
    ):

        @pl.when(near_edge)
        def _():
            clear(xb0, side * (blocks + 1))
            for ref in (meta_h, tiles_h, b_h, u1_h, pick1_h, pick2_h):
                clear(ref, side)

        @pl.when(far_edge)
        def _():
            for ref in (meta_f, far1_h, far2_h):
                clear(ref, side)

    order = [0, blocks - 1] + list(range(1, blocks - 1))
    cells = [slice(g * tile, (g + 1) * tile) for g in range(blocks)]

    loads[0].wait()
    for g in order:
        xb0[g + 1] = u_v[:, cells[g]].astype(BF16)
    loads[1].wait()
    greeted(barrier, 1, 2)
    send(0)
    greet(round_sem.at[0], reaches[0])
    outer = links[0, 2], links[blocks - 1, 1]
    inner = [jnp.clip(link - 1, 0, blocks - 1) for link in outer]
    meta_v[...] = jnp.zeros(meta_v.shape, jnp.int32)
    meta_v[0:blocks] = grp_v[...]
    for side in (0, 1):
        meta_v[blocks + side : blocks + side + 1] = jnp.full((1, tile), outer[side], jnp.int32)
        meta_v[blocks + 2 + side : blocks + 3 + side] = grp_v[pl.ds(inner[side], 1)]
    send(1)
    send(7)

    def own(xb):
        return [dot_nt(xb[g + 1], t_v[g, 0]) for g in range(blocks)]

    def rest(xb, g):
        picked = jnp.concatenate([xb[links[g, 1]], xb[links[g, 2]]], axis=1)
        return dot_nt(picked, jnp.concatenate([t_v[g, 1], t_v[g, 2]], axis=1))

    loads[2].wait()
    send(2)
    loads[3].wait()
    send(3)
    acc = own(xb0)
    scale = [scale_of(t_v[g, 0]) for g in range(blocks)]

    recv(0)
    for g in order:
        new = u_v[:, cells[g]] + (b_v[:, cells[g]] - (acc[g] + rest(xb0, g))) * scale[g]
        u_v[:, cells[g]] = new
        xb1[g + 1] = new.astype(BF16)
        if g == 0:
            u1_e[0] = new
        if g == blocks - 1:
            u1_e[1] = new
            send(6)
            send(4)
    for side in (0, 1):
        pick1[side] = xb1[inner[side] + 1]
    send(5)
    greeted(round_sem.at[0], reaches[0])
    if len(reaches) > 1:
        greet(round_sem.at[1], reaches[1])
    acc = own(xb1)

    for g in range(blocks):
        own_pick[:, cells[g]] = one_hot_t(grp_v[g : g + 1], me * window, tile, window)

    def select(side, own, far, near):
        link = meta_h[side, blocks + 1 - side : blocks + 2 - side]
        mine, beyond = (blocks + 1, 0) if side == 0 else (0, blocks + 1)
        return jnp.where(link == mine, own, jnp.where(link == beyond, far, near))

    def follow(side, xb, field, far, near):
        end, own = xb[side * (blocks + 1)], xb[1 if side == 0 else blocks]
        other = select(side, own.astype(F32), far, near).astype(BF16)
        parts = [end, other, own] if side == 0 else [end, own, other]
        product = dot_nt(
            jnp.concatenate(parts, axis=1),
            jnp.concatenate([tiles_h[side, k] for k in range(3)], axis=1),
        )
        new = field + (b_h[side] - product) * scale_of(tiles_h[side, 0])
        return jnp.where(has_right if side else has_left, new, 0.0)

    for i in (1, 2, 3, 4, 5, 6):
        recv(i)
    for side in (0, 1):
        xb1[side * (blocks + 1)] = u1_h[side].astype(BF16)
    for side in (0, 1):
        new = follow(
            side, xb1, u1_h[side], far1_h[side].astype(F32), pick1_h[side].astype(F32)
        )
        u2_h[side] = new
        xb2[side * (blocks + 1)] = new.astype(BF16)
    for g in order:
        new = u_v[:, cells[g]] + (b_v[:, cells[g]] - (acc[g] + rest(xb1, g))) * scale[g]
        u_v[:, cells[g]] = new
        u2[g] = new
        xb2[g + 1] = new.astype(BF16)
    acc = own(xb2)

    resid = jnp.concatenate(
        [pieces(b_v[:, cells[g]] - (acc[g] + rest(xb2, g)), 3) for g in range(blocks)], axis=1
    )
    sums = unstack(dot_nt(resid, own_pick[...]), 3)
    half = sums.shape[0] // 2
    low = lax.broadcasted_iota(jnp.int32, (half, tile), 1) < window
    odd = lax.rem(me, 2) == 1
    slabs[me] = jnp.where(jnp.logical_xor(low, odd), sums[:half], sums[half:])
    for i in range(1, len(reaches)):
        greeted(round_sem.at[i], reaches[i])
        if i + 1 < len(reaches):
            greet(round_sem.at[i + 1], reaches[i + 1])
    gathers = []
    for off in range(n - 1, 0, -1):
        copy = pltpu.make_async_remote_copy(
            src_ref=slabs.at[me],
            dst_ref=slabs.at[me],
            send_sem=all_send.at[off - 1],
            recv_sem=all_recv.at[off - 1],
            device_id=place(lax.rem(me + off, n)),
            device_id_type=MESH,
        )
        copy.start()
        gathers.append(copy)
    for side in (0, 1):
        pick2[side] = u2[inner[side]]
    send(8)
    send(9)

    for i in (4, 5, 6):
        loads[i].wait()
    flipped = li_v[...].T
    flipped_hi = flipped.astype(BF16)
    flipped_lo = (flipped - flipped_hi.astype(F32)).astype(BF16)
    for m in range(mid_blocks):
        hot = one_hot_t(mg_v[m : m + 1], 0, last, last)
        ct[m] = hot
        e_hi[m] = dot_nn(flipped_hi, hot).astype(BF16)
        e_lo[m] = dot_nn(flipped_lo, hot).astype(BF16)
    mid_scale = [scale_of(mt_v[m, 0]) for m in range(mid_blocks)]
    for g in range(blocks):
        pt[:, cells[g]] = one_hot_t(grp_v[g : g + 1], lax.div(me, 2) * tile, tile, tile)
    recv(7)

    def hot(meta, device):
        return one_hot_t(meta, lax.div(device, 2) * tile, tile, tile)

    beside = ((left, left2, blocks - 1), (right, right2, 0))
    hots = [
        (
            hot(meta_h[side, row : row + 1], near),
            hot(meta_h[side, blocks + 3 - side : blocks + 4 - side], near),
            hot(meta_f[side, row : row + 1], far),
        )
        for side, (near, far, row) in enumerate(beside)
    ]
    for copy in gathers:
        copy.wait_recv()

    side = []
    for m in range(mid_blocks):
        even, other = slabs[2 * m], slabs[2 * m + 1]
        top = jnp.where(low, even, other)
        bottom = pltpu.roll(jnp.where(low, other, even), window, 1)
        side.append(jnp.concatenate([top, bottom], axis=0))

    def mid_apply(values):
        for m in range(mid_blocks):
            mb[m] = values[m].astype(BF16)
        out = []
        for m in range(mid_blocks):
            picked = jnp.concatenate(
                [mb[m], mb[mid_links[m, 1]], mb[mid_links[m, 2]]], axis=1
            )
            out.append(
                dot_nt(picked, jnp.concatenate([mt_v[m, 0], mt_v[m, 1], mt_v[m, 2]], axis=1))
            )
        return out

    def mid_sweep(values):
        return [
            v + (s - a) * d for v, s, a, d in zip(values, side, mid_apply(values), mid_scale)
        ]

    mid = [s * d for s, d in zip(side, mid_scale)]
    mid = mid_sweep(mid)
    mid_resid = [s - a for s, a in zip(side, mid_apply(mid))]
    last_side = dot_nt(pieces(mid_resid[0], 2), ct[0])
    for m in range(1, mid_blocks):
        last_side = last_side + dot_nt(pieces(mid_resid[m], 2), ct[m])
    both = pieces(unstack(last_side, 2), 2)
    high = both[: both.shape[0] // 2]
    mid = [
        mid[m] + (unstack(dot_nn(both, e_hi[m]), 2) + dot_nn(high, e_lo[m]))
        for m in range(mid_blocks)
    ]
    mid = mid_sweep(mid)
    mid = mid_sweep(mid)
    for m in range(mid_blocks):
        mid_v[m] = mid[m]

    def lift(device, hot):
        return unstack(dot_nn(pieces(mid_v[lax.div(device, 2)], 3), hot), 3)

    add = lift(me, pt[...])
    recv(8)
    recv(9)
    u3_h = []
    for side, (near, far, _) in enumerate(beside):
        end = u2_h[side] + lift(near, hots[side][0])
        end = jnp.where(has_right if side else has_left, end, 0.0)
        xb3[side * (blocks + 1)] = end.astype(BF16)
        picked = pick2_h[side] + lift(near, hots[side][1])
        beyond = far2_h[side] + lift(far, hots[side][2])
        beyond = jnp.where(me < n - 2 if side else me > 1, beyond, 0.0)
        u3_h.append((end, beyond, picked))
    for g in range(blocks):
        new = u_v[:, cells[g]] + add[:, cells[g]]
        u_v[:, cells[g]] = new
        xb3[g + 1] = new.astype(BF16)

    acc = own(xb3)
    for side in (0, 1):
        xb4[side * (blocks + 1)] = follow(side, xb3, *u3_h[side]).astype(BF16)
    for g in order:
        new = u_v[:, cells[g]] + (b_v[:, cells[g]] - (acc[g] + rest(xb3, g))) * scale[g]
        u_v[:, cells[g]] = new
        xb4[g + 1] = new.astype(BF16)
    acc = own(xb4)

    for g in range(blocks):
        out_ref[:, cells[g]] = (
            u_v[:, cells[g]] + (b_v[:, cells[g]] - (acc[g] + rest(xb4, g))) * scale[g]
        )
    for i in range(len(swaps)):
        sent(i)
    for copy in gathers:
        copy.wait_send()


def shards(
    right_side,
    start_field,
    fine_tiles,
    fine_links,
    fine_groups,
    mid_tiles,
    mid_links,
    mid_groups,
    last_inverse,
):
    sub = lax.axis_size("sub")
    n = lax.axis_size("rows") * sub
    blocks, _, tile, _ = fine_tiles.shape
    mid_blocks = mid_tiles.shape[0]
    rows = right_side.shape[0]
    last = last_inverse.shape[0]
    anywhere = pl.BlockSpec(memory_space=pltpu.HBM)
    scalars = pl.BlockSpec(memory_space=pltpu.SMEM)
    groups = fine_groups.reshape(blocks, tile)
    mid_groups = mid_groups.reshape(mid_blocks, tile)
    large = [right_side, start_field, fine_tiles, groups, mid_tiles, mid_groups, last_inverse]
    held = pltpu.VMEM((blocks + 2, rows, tile), BF16)
    return pl.pallas_call(
        functools.partial(kernel, n, sub),
        out_shape=jax.ShapeDtypeStruct(right_side.shape, F32),
        in_specs=[scalars] * 2 + [anywhere] * len(large),
        out_specs=pl.BlockSpec(memory_space=pltpu.VMEM),
        scratch_shapes=[pltpu.VMEM(x.shape, x.dtype) for x in large]
        + [held] * 5
        + [
            pltpu.VMEM((blocks + 8, tile), jnp.int32),
            pltpu.VMEM((2, blocks + 8, tile), jnp.int32),
            pltpu.VMEM((2, blocks + 8, tile), jnp.int32),
            pltpu.VMEM((2,) + fine_tiles.shape[1:], BF16),
            pltpu.VMEM((2, rows, tile), F32),
            pltpu.VMEM((2, rows, tile), F32),
            pltpu.VMEM((2, rows, tile), F32),
            pltpu.VMEM((2, rows, tile), BF16),
            pltpu.VMEM((2, rows, tile), BF16),
            pltpu.VMEM((2, rows, tile), BF16),
            pltpu.VMEM((blocks, rows, tile), F32),
            pltpu.VMEM((2, rows, tile), F32),
            pltpu.VMEM((2, rows, tile), F32),
            pltpu.VMEM((2, rows, tile), F32),
            pltpu.VMEM((2, rows, tile), F32),
            pltpu.VMEM((n, rows // 2, tile), F32),
            pltpu.VMEM((tile, blocks * tile), BF16),
            pltpu.VMEM((tile, blocks * tile), BF16),
            pltpu.VMEM((mid_blocks, last, tile), BF16),
            pltpu.VMEM((mid_blocks, last, tile), BF16),
            pltpu.VMEM((mid_blocks, last, tile), BF16),
            pltpu.VMEM((mid_blocks, rows, tile), BF16),
            pltpu.VMEM((mid_blocks, rows, tile), F32),
            pltpu.SemaphoreType.DMA((len(large),)),
            pltpu.SemaphoreType.DMA((10, 2)),
            pltpu.SemaphoreType.DMA((10, 2)),
            pltpu.SemaphoreType.DMA((n - 1,)),
            pltpu.SemaphoreType.DMA((n - 1,)),
            pltpu.SemaphoreType.REGULAR((8,)),
        ],
        compiler_params=pltpu.CompilerParams(
            collective_id=0, has_side_effects=True, vmem_limit_bytes=56308531
        ),
    )(fine_links, mid_links, *large)


def solution(mesh):
    in_specs = (
        P(("parts", "cols"), ("rows", "sub")),
        P(("parts", "cols"), ("rows", "sub")),
        P(("parts", "rows", "sub"), None, None, None),
        P(("parts", "rows", "sub"), None),
        P(("parts", "rows", "sub")),
        P("parts", None, None, None),
        P("parts", None),
        P("parts"),
        P("parts", None),
    )
    out_specs = P(("parts", "cols"), ("rows", "sub"))
    return jax.shard_map(shards, mesh=mesh, in_specs=in_specs, out_specs=out_specs, check_vma=False)
```

```python
import functools

import jax
import jax.numpy as jnp
from jax import lax
from jax.experimental import pallas as pl
from jax.experimental.pallas import tpu as pltpu
from jax.sharding import PartitionSpec as P

damping = 0.6
MESH = pl.DeviceIdType.MESH
F32 = jnp.float32
BF16 = jnp.bfloat16


def dot_nt(a, b):
    return lax.dot_general(a, b, (((1,), (1,)), ((), ())), preferred_element_type=F32)


def dot_nn(a, b):
    return lax.dot_general(a, b, (((1,), (0,)), ((), ())), preferred_element_type=F32)


def pieces(x, count):
    out = []
    for _ in range(count):
        high = x.astype(BF16)
        out.append(high)
        x = x - high.astype(F32)
    return jnp.concatenate(out, axis=0)


def unstack(y, count):
    rows = y.shape[0] // count
    total = y[(count - 1) * rows :]
    for i in range(count - 2, -1, -1):
        total = y[i * rows : (i + 1) * rows] + total
    return total


def one_hot_t(groups, base, rows, period):
    ids = lax.broadcasted_iota(jnp.int32, (rows, groups.shape[1]), 0)
    ids = lax.rem(ids, period) + base
    return jnp.where(ids == groups, 1.0, 0.0).astype(BF16)


def scale_of(tile):
    size = tile.shape[0]
    row = lax.broadcasted_iota(jnp.int32, (size, size), 0)
    col = lax.broadcasted_iota(jnp.int32, (size, size), 1)
    return damping / jnp.sum(jnp.where(row == col, tile.astype(F32), 0.0), axis=0, keepdims=True)


def kernel(
    n,
    sub,
    links_any,
    mid_links_any,
    b_any,
    u_any,
    t_any,
    grp_any,
    mt_any,
    mg_any,
    li_any,
    out_ref,
    b_v,
    u_v,
    t_v,
    grp_v,
    mt_v,
    mg_v,
    li_v,
    xb0,
    xb1,
    xb2,
    xb3,
    xb4,
    meta_v,
    meta_h,
    meta_f,
    tiles_h,
    b_h,
    u1_e,
    u1_h,
    pick1,
    pick1_h,
    far1_h,
    u2,
    u2_h,
    pick2,
    pick2_h,
    far2_h,
    slabs,
    own_pick,
    pt,
    ct,
    e_hi,
    e_lo,
    mb,
    mid_v,
    links,
    mid_links,
    load_sem,
    halo_send,
    halo_recv,
    all_send,
    all_recv,
    round_sem,
):
    blocks, tile = t_v.shape[0], t_v.shape[2]
    mid_blocks = mt_v.shape[0]
    last = li_v.shape[0]
    window = mid_blocks * tile // n
    assert 2 * window == tile
    me = lax.axis_index("rows") * sub + lax.axis_index("sub")
    has_left = me > 0
    has_right = me < n - 1

    def place(j):
        return {"rows": lax.div(j, sub), "sub": lax.rem(j, sub)}

    loads = [
        pltpu.make_async_copy(src, dst, load_sem.at[i])
        for i, (src, dst) in enumerate(
            (
                (u_any, u_v),
                (grp_any, grp_v),
                (t_any, t_v),
                (b_any, b_v),
                (mg_any, mg_v),
                (li_any, li_v),
                (mt_any, mt_v),
                (links_any, links),
                (mid_links_any, mid_links),
            )
        )
    ]
    def greet(sem, distance):
        for there in (me - distance, me + distance):

            @pl.when(jnp.logical_and(there >= 0, there < n))
            def _():
                pl.semaphore_signal(sem, inc=1, device_id=place(there), device_id_type=MESH)

    def greeted(sem, *distances):
        count = jnp.int32(0)
        for distance in distances:
            count = count + jnp.where(me >= distance, 1, 0) + jnp.where(me + distance < n, 1, 0)
        pl.semaphore_wait(sem, count)

    barrier = pltpu.get_barrier_semaphore()
    for distance in (1, 2):
        greet(barrier, distance)
    for load in loads:
        load.start()
    reaches = [2]
    while 2 * reaches[-1] < n - 1:
        reaches.append(2 * reaches[-1])

    left, left2 = jnp.maximum(me - 1, 0), jnp.maximum(me - 2, 0)
    right, right2 = jnp.minimum(me + 1, n - 1), jnp.minimum(me + 2, n - 1)

    def pair(i, first, final, arrived, far=False):
        def copy(src, side, device):
            return pltpu.make_async_remote_copy(
                src_ref=src,
                dst_ref=arrived[1 - side],
                send_sem=halo_send.at[i, side],
                recv_sem=halo_recv.at[i, 1 - side],
                device_id=place(device),
                device_id_type=MESH,
            )

        to_left = copy(first, 0, left2 if far else left)
        to_right = copy(final, 1, right2 if far else right)
        return to_left, to_right, (me > 1 if far else has_left), (me < n - 2 if far else has_right)

    def sides(ref):
        return ref.at[0], ref.at[1]

    edge = slice(0, tile), slice((blocks - 1) * tile, blocks * tile)
    swaps = [
        pair(0, xb0.at[1], xb0.at[blocks], (xb0.at[0], xb0.at[blocks + 1])),
        pair(1, meta_v, meta_v, sides(meta_h)),
        pair(2, t_v.at[0], t_v.at[blocks - 1], sides(tiles_h)),
        pair(3, b_v.at[:, edge[0]], b_v.at[:, edge[1]], sides(b_h)),
        pair(4, u1_e.at[0], u1_e.at[1], sides(u1_h)),
        pair(5, pick1.at[0], pick1.at[1], sides(pick1_h)),
        pair(6, xb1.at[1], xb1.at[blocks], sides(far1_h), far=True),
        pair(7, meta_v, meta_v, sides(meta_f), far=True),
        pair(8, pick2.at[0], pick2.at[1], sides(pick2_h)),
        pair(9, u2.at[0], u2.at[blocks - 1], sides(far2_h), far=True),
    ]

    def send(i):
        to_left, to_right, some_left, some_right = swaps[i]

        @pl.when(some_left)
        def _():
            to_left.start()

        @pl.when(some_right)
        def _():
            to_right.start()

    def recv(i):
        to_left, to_right, some_left, some_right = swaps[i]

        @pl.when(some_left)
        def _():
            to_right.wait_recv()

        @pl.when(some_right)
        def _():
            to_left.wait_recv()

    def sent(i):
        to_left, to_right, some_left, some_right = swaps[i]

        @pl.when(some_left)
        def _():
            to_left.wait_send()

        @pl.when(some_right)
        def _():
            to_right.wait_send()

    def clear(ref, i):
        ref[i] = jnp.zeros(ref.shape[1:], ref.dtype)

    for i in (0, blocks + 1):
        clear(xb1, i)
    for side, near_edge, far_edge in (
        (0, me == 0, me <= 1),
        (1, me == n - 1, me >= n - 2),
    ):

        @pl.when(near_edge)
        def _():
            clear(xb0, side * (blocks + 1))
            for ref in (meta_h, tiles_h, b_h, u1_h, pick1_h, pick2_h):
                clear(ref, side)

        @pl.when(far_edge)
        def _():
            for ref in (meta_f, far1_h, far2_h):
                clear(ref, side)

    order = [0, blocks - 1] + list(range(1, blocks - 1))
    cells = [slice(g * tile, (g + 1) * tile) for g in range(blocks)]

    loads[0].wait()
    for g in order:
        xb0[g + 1] = u_v[:, cells[g]].astype(BF16)
    loads[1].wait()
    greeted(barrier, 1, 2)
    send(0)
    greet(round_sem.at[0], reaches[0])
    loads[7].wait()
    outer = links[0, 2], links[blocks - 1, 1]
    inner = [jnp.clip(link - 1, 0, blocks - 1) for link in outer]
    meta_v[...] = jnp.zeros(meta_v.shape, jnp.int32)
    meta_v[0:blocks] = grp_v[...]
    for side in (0, 1):
        meta_v[blocks + side : blocks + side + 1] = jnp.full((1, tile), outer[side], jnp.int32)
        meta_v[blocks + 2 + side : blocks + 3 + side] = grp_v[pl.ds(inner[side], 1)]
    send(1)
    send(7)

    def own(xb):
        return [dot_nt(xb[g + 1], t_v[g, 0]) for g in range(blocks)]

    def rest(xb, g):
        picked = jnp.concatenate([xb[links[g, 1]], xb[links[g, 2]]], axis=1)
        return dot_nt(picked, jnp.concatenate([t_v[g, 1], t_v[g, 2]], axis=1))

    loads[2].wait()
    send(2)
    loads[3].wait()
    send(3)
    acc = own(xb0)
    scale = [scale_of(t_v[g, 0]) for g in range(blocks)]

    recv(0)
    for g in order:
        new = u_v[:, cells[g]] + (b_v[:, cells[g]] - (acc[g] + rest(xb0, g))) * scale[g]
        u_v[:, cells[g]] = new
        xb1[g + 1] = new.astype(BF16)
        if g == 0:
            u1_e[0] = new
        if g == blocks - 1:
            u1_e[1] = new
            send(6)
            send(4)
    for side in (0, 1):
        pick1[side] = xb1[inner[side] + 1]
    send(5)
    greeted(round_sem.at[0], reaches[0])
    if len(reaches) > 1:
        greet(round_sem.at[1], reaches[1])
    acc = own(xb1)

    for g in range(blocks):
        own_pick[:, cells[g]] = one_hot_t(grp_v[g : g + 1], me * window, tile, window)

    def select(side, own, far, near):
        link = meta_h[side, blocks + 1 - side : blocks + 2 - side]
        mine, beyond = (blocks + 1, 0) if side == 0 else (0, blocks + 1)
        return jnp.where(link == mine, own, jnp.where(link == beyond, far, near))

    def follow(side, xb, field, far, near):
        end, own = xb[side * (blocks + 1)], xb[1 if side == 0 else blocks]
        other = select(side, own.astype(F32), far, near).astype(BF16)
        parts = [end, other, own] if side == 0 else [end, own, other]
        product = dot_nt(
            jnp.concatenate(parts, axis=1),
            jnp.concatenate([tiles_h[side, k] for k in range(3)], axis=1),
        )
        new = field + (b_h[side] - product) * scale_of(tiles_h[side, 0])
        return jnp.where(has_right if side else has_left, new, 0.0)

    for i in (1, 2, 3, 4, 5, 6):
        recv(i)
    for side in (0, 1):
        xb1[side * (blocks + 1)] = u1_h[side].astype(BF16)
    for side in (0, 1):
        new = follow(
            side, xb1, u1_h[side], far1_h[side].astype(F32), pick1_h[side].astype(F32)
        )
        u2_h[side] = new
        xb2[side * (blocks + 1)] = new.astype(BF16)
    for g in order:
        new = u_v[:, cells[g]] + (b_v[:, cells[g]] - (acc[g] + rest(xb1, g))) * scale[g]
        u_v[:, cells[g]] = new
        u2[g] = new
        xb2[g + 1] = new.astype(BF16)
    acc = own(xb2)

    resid = jnp.concatenate(
        [pieces(b_v[:, cells[g]] - (acc[g] + rest(xb2, g)), 3) for g in range(blocks)], axis=1
    )
    sums = unstack(dot_nt(resid, own_pick[...]), 3)
    half = sums.shape[0] // 2
    low = lax.broadcasted_iota(jnp.int32, (half, tile), 1) < window
    odd = lax.rem(me, 2) == 1
    slabs[me] = jnp.where(jnp.logical_xor(low, odd), sums[:half], sums[half:])
    for i in range(1, len(reaches)):
        greeted(round_sem.at[i], reaches[i])
        if i + 1 < len(reaches):
            greet(round_sem.at[i + 1], reaches[i + 1])
    gathers = []
    for off in range(n - 1, 0, -1):
        copy = pltpu.make_async_remote_copy(
            src_ref=slabs.at[me],
            dst_ref=slabs.at[me],
            send_sem=all_send.at[off - 1],
            recv_sem=all_recv.at[off - 1],
            device_id=place(lax.rem(me + off, n)),
            device_id_type=MESH,
        )
        copy.start()
        gathers.append(copy)
    for side in (0, 1):
        pick2[side] = u2[inner[side]]
    send(8)
    send(9)

    for i in (4, 5, 6, 8):
        loads[i].wait()
    flipped = li_v[...].T
    flipped_hi = flipped.astype(BF16)
    flipped_lo = (flipped - flipped_hi.astype(F32)).astype(BF16)
    for m in range(mid_blocks):
        hot = one_hot_t(mg_v[m : m + 1], 0, last, last)
        ct[m] = hot
        e_hi[m] = dot_nn(flipped_hi, hot).astype(BF16)
        e_lo[m] = dot_nn(flipped_lo, hot).astype(BF16)
    mid_scale = [scale_of(mt_v[m, 0]) for m in range(mid_blocks)]
    for g in range(blocks):
        pt[:, cells[g]] = one_hot_t(grp_v[g : g + 1], lax.div(me, 2) * tile, tile, tile)
    recv(7)

    def hot(meta, device):
        return one_hot_t(meta, lax.div(device, 2) * tile, tile, tile)

    beside = ((left, left2, blocks - 1), (right, right2, 0))
    hots = [
        (
            hot(meta_h[side, row : row + 1], near),
            hot(meta_h[side, blocks + 3 - side : blocks + 4 - side], near),
            hot(meta_f[side, row : row + 1], far),
        )
        for side, (near, far, row) in enumerate(beside)
    ]
    for copy in gathers:
        copy.wait_recv()

    side = []
    for m in range(mid_blocks):
        even, other = slabs[2 * m], slabs[2 * m + 1]
        top = jnp.where(low, even, other)
        bottom = pltpu.roll(jnp.where(low, other, even), window, 1)
        side.append(jnp.concatenate([top, bottom], axis=0))

    def mid_apply(values):
        for m in range(mid_blocks):
            mb[m] = values[m].astype(BF16)
        out = []
        for m in range(mid_blocks):
            picked = jnp.concatenate(
                [mb[m], mb[mid_links[m, 1]], mb[mid_links[m, 2]]], axis=1
            )
            out.append(
                dot_nt(picked, jnp.concatenate([mt_v[m, 0], mt_v[m, 1], mt_v[m, 2]], axis=1))
            )
        return out

    def mid_sweep(values):
        return [
            v + (s - a) * d for v, s, a, d in zip(values, side, mid_apply(values), mid_scale)
        ]

    mid = [s * d for s, d in zip(side, mid_scale)]
    mid = mid_sweep(mid)
    mid_resid = [s - a for s, a in zip(side, mid_apply(mid))]
    last_side = dot_nt(pieces(mid_resid[0], 2), ct[0])
    for m in range(1, mid_blocks):
        last_side = last_side + dot_nt(pieces(mid_resid[m], 2), ct[m])
    both = pieces(unstack(last_side, 2), 2)
    high = both[: both.shape[0] // 2]
    mid = [
        mid[m] + (unstack(dot_nn(both, e_hi[m]), 2) + dot_nn(high, e_lo[m]))
        for m in range(mid_blocks)
    ]
    mid = mid_sweep(mid)
    mid = mid_sweep(mid)
    for m in range(mid_blocks):
        mid_v[m] = mid[m]

    def lift(device, hot):
        return unstack(dot_nn(pieces(mid_v[lax.div(device, 2)], 3), hot), 3)

    add = lift(me, pt[...])
    recv(8)
    recv(9)
    u3_h = []
    for side, (near, far, _) in enumerate(beside):
        end = u2_h[side] + lift(near, hots[side][0])
        end = jnp.where(has_right if side else has_left, end, 0.0)
        xb3[side * (blocks + 1)] = end.astype(BF16)
        picked = pick2_h[side] + lift(near, hots[side][1])
        beyond = far2_h[side] + lift(far, hots[side][2])
        beyond = jnp.where(me < n - 2 if side else me > 1, beyond, 0.0)
        u3_h.append((end, beyond, picked))
    for g in range(blocks):
        new = u_v[:, cells[g]] + add[:, cells[g]]
        u_v[:, cells[g]] = new
        xb3[g + 1] = new.astype(BF16)

    acc = own(xb3)
    for side in (0, 1):
        xb4[side * (blocks + 1)] = follow(side, xb3, *u3_h[side]).astype(BF16)
    for g in order:
        new = u_v[:, cells[g]] + (b_v[:, cells[g]] - (acc[g] + rest(xb3, g))) * scale[g]
        u_v[:, cells[g]] = new
        xb4[g + 1] = new.astype(BF16)
    acc = own(xb4)

    for g in range(blocks):
        out_ref[:, cells[g]] = (
            u_v[:, cells[g]] + (b_v[:, cells[g]] - (acc[g] + rest(xb4, g))) * scale[g]
        )
    for i in range(len(swaps)):
        sent(i)
    for copy in gathers:
        copy.wait_send()


def shards(
    right_side,
    start_field,
    fine_tiles,
    fine_links,
    fine_groups,
    mid_tiles,
    mid_links,
    mid_groups,
    last_inverse,
):
    sub = lax.axis_size("sub")
    n = lax.axis_size("rows") * sub
    blocks, _, tile, _ = fine_tiles.shape
    mid_blocks = mid_tiles.shape[0]
    rows = right_side.shape[0]
    last = last_inverse.shape[0]
    anywhere = pl.BlockSpec(memory_space=pltpu.HBM)
    groups = fine_groups.reshape(blocks, tile)
    mid_groups = mid_groups.reshape(mid_blocks, tile)
    large = [right_side, start_field, fine_tiles, groups, mid_tiles, mid_groups, last_inverse]
    held = pltpu.VMEM((blocks + 2, rows, tile), BF16)
    return pl.pallas_call(
        functools.partial(kernel, n, sub),
        out_shape=jax.ShapeDtypeStruct(right_side.shape, F32),
        in_specs=[anywhere] * (2 + len(large)),
        out_specs=pl.BlockSpec(memory_space=pltpu.VMEM),
        scratch_shapes=[pltpu.VMEM(x.shape, x.dtype) for x in large]
        + [held] * 5
        + [
            pltpu.VMEM((blocks + 8, tile), jnp.int32),
            pltpu.VMEM((2, blocks + 8, tile), jnp.int32),
            pltpu.VMEM((2, blocks + 8, tile), jnp.int32),
            pltpu.VMEM((2,) + fine_tiles.shape[1:], BF16),
            pltpu.VMEM((2, rows, tile), F32),
            pltpu.VMEM((2, rows, tile), F32),
            pltpu.VMEM((2, rows, tile), F32),
            pltpu.VMEM((2, rows, tile), BF16),
            pltpu.VMEM((2, rows, tile), BF16),
            pltpu.VMEM((2, rows, tile), BF16),
            pltpu.VMEM((blocks, rows, tile), F32),
            pltpu.VMEM((2, rows, tile), F32),
            pltpu.VMEM((2, rows, tile), F32),
            pltpu.VMEM((2, rows, tile), F32),
            pltpu.VMEM((2, rows, tile), F32),
            pltpu.VMEM((n, rows // 2, tile), F32),
            pltpu.VMEM((tile, blocks * tile), BF16),
            pltpu.VMEM((tile, blocks * tile), BF16),
            pltpu.VMEM((mid_blocks, last, tile), BF16),
            pltpu.VMEM((mid_blocks, last, tile), BF16),
            pltpu.VMEM((mid_blocks, last, tile), BF16),
            pltpu.VMEM((mid_blocks, rows, tile), BF16),
            pltpu.VMEM((mid_blocks, rows, tile), F32),
            pltpu.SMEM(fine_links.shape, jnp.int32),
            pltpu.SMEM(mid_links.shape, jnp.int32),
            pltpu.SemaphoreType.DMA((2 + len(large),)),
            pltpu.SemaphoreType.DMA((10, 2)),
            pltpu.SemaphoreType.DMA((10, 2)),
            pltpu.SemaphoreType.DMA((n - 1,)),
            pltpu.SemaphoreType.DMA((n - 1,)),
            pltpu.SemaphoreType.REGULAR((8,)),
        ],
        compiler_params=pltpu.CompilerParams(
            collective_id=0, has_side_effects=True, vmem_limit_bytes=56308531
        ),
    )(fine_links, mid_links, *large)


def solution(mesh):
    in_specs = (
        P(("parts", "cols"), ("rows", "sub")),
        P(("parts", "cols"), ("rows", "sub")),
        P(("parts", "rows", "sub"), None, None, None),
        P(("parts", "rows", "sub"), None),
        P(("parts", "rows", "sub")),
        P("parts", None, None, None),
        P("parts", None),
        P("parts"),
        P("parts", None),
    )
    out_specs = P(("parts", "cols"), ("rows", "sub"))
    return jax.shard_map(shards, mesh=mesh, in_specs=in_specs, out_specs=out_specs, check_vma=False)
```
